32 devices in a mesh: batch: 16 (over z, y, core), seq: 2 (over x).
Axes of the slice: x: 2, y: 2, z: 4, core: 2. Of those that a mesh axis runs over, the one named last changes fastest.
Arguments:
- hidden_in: bfloat16 [32, 256, 512], P('batch', 'seq'), may hold values from -6 to 6
- memory: bfloat16 [32, 512, 512], P('batch', 'seq'), may hold values from -6 to 6
- target_lengths: int32 [32], P('batch'), may hold values from 76 to 230, as said below
- source_mask: int32 [32, 512], P('batch'), may hold values 0 or 1
- grad_out: bfloat16 [32, 256, 512], P('batch', 'seq'), may hold values from -6 to 6
- attn_qkv: bfloat16 [512, 1536], P(('batch', 'seq')), may hold values from -0.25 to 0.25
- attn_out: bfloat16 [512, 512], P(('batch', 'seq')), may hold values from -1 to 1
- cross_q: bfloat16 [512, 512], P(('batch', 'seq')), may hold values from -0.25 to 0.25
- cross_kv: bfloat16 [512, 1024], P(('batch', 'seq')), may hold values from -0.25 to 0.25
- cross_out: bfloat16 [512, 512], P(('batch', 'seq')), may hold values from -1 to 1
- ffn_up: bfloat16 [512, 2048], P(('batch', 'seq')), may hold values from -0.25 to 0.25
- ffn_down: bfloat16 [2048, 512], P(('batch', 'seq')), may hold values from -0.125 to 0.125
- gains: bfloat16 [512, 3], P(('batch', 'seq')), may hold values from 0.5 to 1.5
- biases: bfloat16 [512, 10], P(('batch', 'seq')), may hold values from -1.796875 to 1.796875
- ffn_bias: bfloat16 [2048], P(('batch', 'seq')), may hold values from -1.796875 to 1.796875
Outputs:
- output: bfloat16 [32, 256, 512], P('batch', 'seq')
- grad_hidden_in: float32 [32, 256, 512], P('batch', 'seq')
- grad_memory: float32 [32, 512, 512], P('batch', 'seq')
- grad_attn_qkv: float32 [512, 1536], P(('batch', 'seq'))
- grad_attn_out: float32 [512, 512], P(('batch', 'seq'))
- grad_cross_q: float32 [512, 512], P(('batch', 'seq'))
- grad_cross_kv: float32 [512, 1024], P(('batch', 'seq'))
- grad_cross_out: float32 [512, 512], P(('batch', 'seq'))
- grad_ffn_up: float32 [512, 2048], P(('batch', 'seq'))
- grad_ffn_down: float32 [2048, 512], P(('batch', 'seq'))
- grad_gains: float32 [512, 3], P(('batch', 'seq'))
- grad_biases: float32 [512, 10], P(('batch', 'seq'))
- grad_ffn_bias: float32 [2048], P(('batch', 'seq'))
The draws below stay inside these ranges and needn't reach their ends.
Inputs may be any that keep to these rules, and one draw needn't show every extreme that they name: `target_lengths`: in each aligned block of 2 examples (one index of batch) some example has a target length above 128.
All inputs are finite; a program needn't handle non-finite values. No bound on the sum of `source_mask` on one device may be relied on, other than what follows from the above.
Results may differ from the reference program's by a relative error of at most 0.015.
Values may be sent and summed in bfloat16 or wider, within the bound.
No kernel may reach another device: no remote copies, remote signals or barrier semaphores. Data moves between devices by JAX's collectives and lax.ppermute only.
A program may use at most 128 MiB of HBM per device.

```python
import math
from functools import partial
import jax
import jax.numpy as jnp
from jax import lax

D = 512
HEADS = 8
HEAD_DIM = 64
FF = 2048
EX_DEV = 2
TGT = 256
SRC = 512
EX = 32


def draw_target_lengths(key, part):
    key = jax.random.fold_in(key, 11)
    key_base, key_pick, key_long = jax.random.split(key, 3)
    shortest = 3 * TGT // 10
    longest = 9 * TGT // 10
    block_count = EX // EX_DEV
    base_lengths = jax.random.randint(key_base, (block_count, EX_DEV), shortest, longest + 1)
    chosen = jax.random.randint(key_pick, (block_count, 1), 0, EX_DEV)
    picked_slot = jnp.arange(EX_DEV)[None, :] == chosen
    long_lengths = jax.random.randint(key_long, (block_count, EX_DEV), TGT // 2 + 1, longest + 1)
    return jnp.where(picked_slot, long_lengths, base_lengths).reshape(EX).astype(jnp.int32)


def plant(values, own_key, least, largest):
    spot = [jax.random.randint(jax.random.fold_in(own_key, axis), (), 0, length) for axis, length in enumerate(values.shape)]
    widest = values.shape.index(max(values.shape))
    next_to = spot[:widest] + [(spot[widest] + 1) % values.shape[widest]] + spot[widest + 1:]
    return values.at[tuple(spot)].set(least).at[tuple(next_to)].set(largest)


def block_levels(key, dims, cuts, low, top_value):
    factor_of, own = 1.0, jax.random.fold_in(key, 6)
    for position, blocks in cuts:
        draws = jnp.exp(jax.random.uniform(jax.random.fold_in(own, position), (blocks,), jnp.float32, low / len(cuts), top_value / len(cuts)))
        factor_of = factor_of * jnp.repeat(draws, dims[position] // blocks).reshape([-1 if axis == position else 1 for axis in range(len(dims))])
    return factor_of


def bell_draw(own_key, extent, spread, most, cuts=(), held_as=jnp.bfloat16):
    values = spread * jax.random.normal(own_key, extent, jnp.float32)
    if cuts:
        values = values * block_levels(own_key, extent, cuts, -0.22, 0.18)
    return jnp.clip(values, -most, most).astype(held_as)


def setup_inputs(seed: int = 0) -> dict:
    keys = jax.random.split(jax.random.key(seed), 16)
    return {
        "hidden_in": bell_draw(keys[0], (EX, TGT, D), 1.0, 6.0, ((0, 16), (1, 2))),
        "memory": bell_draw(keys[1], (EX, SRC, D), 1.0, 6.0, ((0, 16), (1, 2))),
        "target_lengths": draw_target_lengths(jax.random.fold_in(keys[15], 71), 0),
        "source_mask": plant((jax.random.randint(keys[3], (EX, SRC), 0, 8) < 7).astype(jnp.int32), jax.random.fold_in(keys[3], 1), 0, 1),
        "grad_out": bell_draw(keys[4], (EX, TGT, D), 1.0, 6.0, ((0, 16), (1, 2))),
        "attn_qkv": bell_draw(keys[5], (D, 3 * D), D ** -0.5, 0.25, ((0, 32),)),
        "attn_out": bell_draw(keys[6], (D, D), (D // 16) ** -0.5, 1.0, ((0, 32),)),
        "cross_q": bell_draw(keys[7], (D, D), D ** -0.5, 0.25, ((0, 32),)),
        "cross_kv": bell_draw(keys[8], (D, 2 * D), D ** -0.5, 0.25, ((0, 32),)),
        "cross_out": bell_draw(keys[9], (D, D), (D // 16) ** -0.5, 1.0, ((0, 32),)),
        "ffn_up": bell_draw(keys[10], (D, FF), D ** -0.5, 0.25, ((0, 32),)),
        "ffn_down": bell_draw(keys[11], (FF, D), FF ** -0.5, 0.125, ((0, 32),)),
        "gains": jnp.clip(1.0 + 0.1 * jax.random.normal(keys[12], (D, 3), jnp.float32), 0.5, 1.5).astype(jnp.bfloat16),
        "biases": bell_draw(keys[13], (D, 10), 0.3, 1.796875, ((0, 32),)),
        "ffn_bias": bell_draw(keys[14], (FF,), 0.3, 1.796875, ((0, 32),)),
    }


@jax.custom_vjp
def low(v):
    return lax.optimization_barrier(v.astype(jnp.bfloat16)).astype(jnp.float32)

@jax.custom_vjp
def low_back(v):
    return v

def low_keep(v):
    return (low(v), None)

def low_pass(kept, grad):
    return (grad,)

def back_keep(v):
    return (v, None)

def back_low(kept, grad):
    return (low(grad),)
low.defvjp(low_keep, low_pass)
low_back.defvjp(back_keep, back_low)
EPSILON = 1e-05
NEGATIVE = -1000000000.0
HIGHEST = lax.Precision.HIGHEST

def layer_norm(values, gain, shift):
    centred = values - lax.optimization_barrier(jnp.mean(values, axis=-1, keepdims=True))
    variance = lax.optimization_barrier(jnp.mean(centred * centred, axis=-1, keepdims=True))
    return centred * lax.rsqrt(variance + EPSILON) * gain + shift

def project(left, weight):
    return jnp.einsum('gtd,df->gtf', left, weight, precision=HIGHEST)

def split_heads(values):
    return values.reshape(values.shape[0], values.shape[1], HEADS, HEAD_DIM)

def attend(queries, key_rows, values, visible):
    scores = jnp.einsum('gqhc,gkhc->ghqk', split_heads(queries), split_heads(key_rows), precision=HIGHEST) * HEAD_DIM ** (-0.5)
    scores = low_back(jnp.where(visible[:, None], scores, NEGATIVE))
    row_max = lax.optimization_barrier(jnp.max(scores, axis=-1, keepdims=True))
    exponent = jnp.exp(scores - row_max)
    attn_weights = low(exponent / lax.optimization_barrier(jnp.sum(exponent, axis=-1, keepdims=True)))
    mixed = jnp.einsum('ghqk,gkhc->gqhc', attn_weights, split_heads(values), precision=HIGHEST)
    return low_back(low(mixed.reshape(queries.shape)))

def layer_block(weight_set, hidden_in, memory, self_visible, cross_visible):
    w_qkv, w_out, w_cq, w_ckv, w_co, w_up, w_down, gain_cols, bias_cols, bias_up = weight_set
    model_width = hidden_in.shape[-1]
    normed1 = low(layer_norm(hidden_in, gain_cols[:, 0], bias_cols[:, 0]))
    joined_proj = project(normed1, w_qkv)
    queries = low_back(low(joined_proj[..., :model_width] + bias_cols[:, 1]))
    key_rows = low_back(low(joined_proj[..., model_width:2 * model_width]))
    values = low_back(low(joined_proj[..., 2 * model_width:] + bias_cols[:, 2]))
    mixed1 = attend(queries, key_rows, values, self_visible)
    after_self = hidden_in + low_back(project(mixed1, w_out) + bias_cols[:, 3])
    normed2 = low(layer_norm(after_self, gain_cols[:, 1], bias_cols[:, 4]))
    cross_queries = low_back(low(project(normed2, w_cq) + bias_cols[:, 5]))
    cross_proj = project(memory, w_ckv)
    cross_keys = low_back(low(cross_proj[..., :model_width]))
    cross_values = low_back(low(cross_proj[..., model_width:] + bias_cols[:, 6]))
    mixed2 = attend(cross_queries, cross_keys, cross_values, cross_visible)
    after_cross = after_self + low_back(project(mixed2, w_co) + bias_cols[:, 7])
    normed3 = low(layer_norm(after_cross, gain_cols[:, 2], bias_cols[:, 8]))
    hidden = low_back(project(normed3, w_up) + bias_up)
    active = low(jax.nn.gelu(hidden))
    return after_cross + low_back(project(active, w_down) + bias_cols[:, 9])

def reference(hidden_in, memory, target_lengths, source_mask, grad_out, attn_qkv, attn_out, cross_q, cross_kv, cross_out, ffn_up, ffn_down, gains, biases, ffn_bias):
    positions = jnp.arange(TGT)
    self_visible = (positions[None, None, :] <= positions[None, :, None]) & (positions[None, None, :] < target_lengths[:, None, None])
    cross_visible = ((source_mask > 0) | (jnp.arange(SRC) == 0)[None, :])[:, None, :]
    weight_set = tuple((matrix.astype(jnp.float32) for matrix in (attn_qkv, attn_out, cross_q, cross_kv, cross_out, ffn_up, ffn_down, gains, biases, ffn_bias)))
    group_size = math.gcd(EX, max(1, 4096 // TGT))
    group_count = EX // group_size

    def to_groups(array):
        return array.reshape((group_count, group_size) + array.shape[1:])

    def forward(hidden_float, memory_float, weight_tuple):
        block_fn = jax.checkpoint(partial(layer_block, weight_tuple))

        def scan_body(unused_carry, slices):
            return (unused_carry, block_fn(*slices))
        _, outputs = lax.scan(scan_body, jnp.zeros((), jnp.float32), (to_groups(hidden_float), to_groups(memory_float), to_groups(self_visible), to_groups(cross_visible)))
        return outputs.reshape(hidden_float.shape)
    output, backward = jax.vjp(forward, hidden_in.astype(jnp.float32), memory.astype(jnp.float32), weight_set)
    grad_hidden, grad_memory, grad_weights = backward(grad_out.astype(jnp.float32))
    return (output.astype(jnp.bfloat16), grad_hidden, grad_memory, grad_weights[0], grad_weights[1], grad_weights[2], grad_weights[3], grad_weights[4], grad_weights[5], grad_weights[6], grad_weights[7], grad_weights[8], grad_weights[9])
```

```python
import functools

import jax
import jax.numpy as jnp
from jax import lax
from jax.experimental import pallas as pl
from jax.experimental.pallas import tpu as pltpu
from jax.sharding import PartitionSpec as P

D = 512
FF = 2048
HEADS = 8
HEAD_DIM = 64
EPSILON = 1e-05
NEGATIVE = -1000000000.0
SCALE = HEAD_DIM ** (-0.5)
BLOCKS = 32
WIDE = 4096
BF = jnp.bfloat16
F32 = jnp.float32
BOTH = ("batch", "seq")

QKV, OUT, CQ, CKV, CO = (0, 1536), (1536, 2048), (2048, 2560), (2560, 3584), (3584, 4096)


def dot(a, b):
    return lax.dot_general(a, b, (((1,), (0,)), ((), ())), preferred_element_type=F32)


def dot_nt(a, b):
    return lax.dot_general(a, b, (((1,), (1,)), ((), ())), preferred_element_type=F32)


def dot_tn(a, b):
    return lax.dot_general(a, b, (((0,), (0,)), ((), ())), preferred_element_type=F32)


def norm(values):
    centred = values - jnp.mean(values, axis=-1, keepdims=True)
    rate = lax.rsqrt(jnp.mean(centred * centred, axis=-1, keepdims=True) + EPSILON)
    return centred * rate, rate


def norm_back(values, gain, grad):
    unit, rate = norm(values)
    scaled = grad * gain
    part = rate * (
        scaled
        - jnp.mean(scaled, axis=-1, keepdims=True)
        - unit * jnp.mean(scaled * unit, axis=-1, keepdims=True)
    )
    return part, row_sum(grad * unit), row_sum(grad)


def row_sum(values):
    return jnp.sum(values.astype(F32), axis=0, keepdims=True)


def lane_masks(dtype):
    lane = lax.broadcasted_iota(jnp.int32, (1, 128), 1)
    return [(lane // HEAD_DIM == j).astype(dtype) for j in range(2)]


def scores_t(keys, queries, visible):
    return jnp.where(visible, dot_nt(keys, queries) * SCALE, NEGATIVE)


def attend(q_ref, k_ref, v_ref, visible, mixed_ref, log_ref):
    masks = lane_masks(BF)
    for pair in range(HEADS // 2):
        cols = slice(128 * pair, 128 * pair + 128)
        queries, keys, values = q_ref[:, cols], k_ref[:, cols], v_ref[:, cols]
        total = None
        for j in range(2):
            scores = scores_t(keys, queries * masks[j], visible)
            top = jnp.max(scores, axis=0, keepdims=True)
            exponent = jnp.exp(scores - top)
            row_total = jnp.sum(exponent, axis=0, keepdims=True)
            probs = (exponent * (1.0 / row_total)).astype(BF)
            log_ref[2 * pair + j : 2 * pair + j + 1, :] = top + jnp.log(row_total)
            part = dot_tn(probs, values * masks[j])
            total = part if total is None else total + part
        mixed_ref[:, cols] = total.astype(BF)


def attend_back(q_ref, k_ref, v_ref, visible, log_ref, grad_ref, dq_ref, dk_ref, dv_ref):
    masks = lane_masks(BF)
    for pair in range(HEADS // 2):
        cols = slice(128 * pair, 128 * pair + 128)
        queries, keys, values, grads = q_ref[:, cols], k_ref[:, cols], v_ref[:, cols], grad_ref[:, cols]
        dq = dk = dv = None
        for j in range(2):
            own_q, own_k, own_g = queries * masks[j], keys * masks[j], grads * masks[j]
            scores = scores_t(keys, own_q, visible)
            probs = jnp.exp(scores - log_ref[2 * pair + j : 2 * pair + j + 1, :])
            grad_probs = dot_nt(values, own_g)
            part_v = dot(probs.astype(BF), own_g)
            inner = jnp.sum(probs * grad_probs, axis=0, keepdims=True)
            low = (probs * (grad_probs - inner)).astype(BF)
            part_k = dot(low, own_q)
            part_q = dot_tn(low, own_k)
            dq = part_q if dq is None else dq + part_q
            dk = part_k if dk is None else dk + part_k
            dv = part_v if dv is None else dv + part_v
        dq_ref[:, cols] = (dq * SCALE).astype(BF)
        dk_ref[:, cols] = (dk * SCALE).astype(BF)
        dv_ref[:, cols] = dv.astype(BF)


def copies_in(order, pieces, pairs, sems):
    started, slot = [], 0
    first = 0
    for piece in pieces:
        for k in range(piece.shape[0]):
            for source, target in pairs(piece, k, order[first + k]):
                copy = pltpu.make_async_copy(source, target, sems.at[slot])
                copy.start()
                started.append(copy)
                slot += 1
        first += piece.shape[0]
    return started


def copies_out(order, outs, pairs, sems):
    return copies_in(order, outs, lambda out, k, index: [(b, a) for a, b in pairs(out, k, index)], sems)


def wait_all(started):
    for copy in started:
        copy.wait()


def rows16(index):
    return pl.ds(pl.multiple_of(index * 16, 16), 16)


def halves(ref, place, rows):
    own = pl.ds(pl.multiple_of(place * rows, rows), rows)
    other = pl.ds(pl.multiple_of((1 - place) * rows, rows), rows)
    return ref.at[own], ref.at[other]


def self_visible(length, rows):
    key = lax.broadcasted_iota(jnp.int32, (rows, rows), 0)
    query = lax.broadcasted_iota(jnp.int32, (rows, rows), 1)
    return (key <= query) & (key < length)


def forward_kernel(
    n_pieces, order, info, *refs
):
    pieces = refs[:n_pieces]
    (h_own, h_new, m_own, m_new, mask) = refs[n_pieces : n_pieces + 5]
    (
        x0, mem, normed1, q, k, v, mixed1, log1, x1, normed2, cq, ck, cv, mixed2, log2, x2, normed3, vecs, ffb,
        weights, small, sems, sems2,
    ) = refs[n_pieces + 5 :]
    place, length = info[0], info[1]
    started = copies_in(
        order,
        pieces,
        lambda piece, b, index: [(piece.at[b, :, 0:WIDE], weights.at[rows16(index)])],
        sems,
    )
    started += copies_in(
        order, pieces, lambda piece, b, index: [(piece.at[b, :, WIDE : WIDE + 128], small.at[index])], sems2
    )
    rows = h_own.shape[0]
    own, new = halves(x0, place, rows)
    own[...], new[...] = h_own[...], h_new[...]
    own, new = halves(mem, place, m_own.shape[0])
    own[...], new[...] = m_own[...], m_new[...]
    hidden = x0[...].astype(F32)
    unit1, _ = norm(hidden)
    wait_all(started)

    lane = lax.broadcasted_iota(jnp.int32, (16, 128), 1)
    for tile in range(D // 128):
        row = jnp.zeros((16, 128), F32)
        for i in range(8):
            row = jnp.where(lane // 16 == i, small[8 * tile + i].astype(F32), row)
        vecs[:, 128 * tile : 128 * tile + 128] = row
    ffb[...] = jnp.zeros_like(ffb)
    for tile in range(FF // 128):
        row = jnp.where(lane < 64, small[2 * tile].astype(F32), small[2 * tile + 1].astype(F32))
        ffb[tile // 4 : tile // 4 + 1, 128 * (tile % 4) : 128 * (tile % 4) + 128] = row[13:14, :]

    def bias(j):
        return vecs[j : j + 1, :]

    normed1[...] = (unit1 * bias(10) + bias(0)).astype(BF)
    q[...] = (dot(normed1[...], weights[:, 0:512]) + bias(1)).astype(BF)
    k[...] = dot(normed1[...], weights[:, 512:1024]).astype(BF)
    v[...] = (dot(normed1[...], weights[:, 1024:1536]) + bias(2)).astype(BF)
    ck[...] = dot(mem[...], weights[:, 2560:3072]).astype(BF)
    cv[...] = (dot(mem[...], weights[:, 3072:3584]) + bias(6)).astype(BF)
    attend(q, k, v, self_visible(length, 2 * rows), mixed1, log1)
    after_self = hidden + (dot(mixed1[...], weights[:, OUT[0] : OUT[1]]) + bias(3))
    x1[...] = after_self
    normed2[...] = (norm(after_self)[0] * bias(11) + bias(4)).astype(BF)
    cq[...] = (dot(normed2[...], weights[:, CQ[0] : CQ[1]]) + bias(5)).astype(BF)
    attend(cq, ck, cv, mask[...] > 0, mixed2, log2)
    after_cross = after_self + (dot(mixed2[...], weights[:, CO[0] : CO[1]]) + bias(7))
    x2[...] = after_cross
    normed3[...] = (norm(after_cross)[0] * bias(12) + bias(8)).astype(BF)


def ffn_kernel(n_pieces, n_outs, order, info, *refs):
    pieces = refs[:n_pieces]
    (x2, normed3, g_own, g_new, vecs, ffb) = refs[n_pieces : n_pieces + 6]
    rest = refs[n_pieces + 6 :]
    (out_keep, out_send, grad_x2, small, ffg) = rest[:5]
    outs = rest[5 : 5 + n_outs]
    (up, down, d_up, d_down, grad_out, sems) = rest[5 + n_outs :]
    place = info[0]

    def down_rows(index):
        return pl.ds(pl.multiple_of(index * 4, 4), 4)

    wait = copies_in(
        order,
        pieces,
        lambda piece, b, index: [
            (piece.at[b, 0:4], up.at[:, rows16(index)]),
            (piece.at[b, 4:8], down.at[down_rows(index)]),
        ],
        sems,
    )
    rows = g_own.shape[0]
    own, new = halves(grad_out, place, rows)
    own[...], new[...] = g_own[...], g_new[...]
    wait_all(wait)
    grads = grad_out[...]
    normed = normed3[...]
    normed_t = normed.T
    result = None
    grad_normed = None
    c0 = (2.0 / jnp.pi) ** 0.5
    ffg[...] = jnp.zeros_like(ffg)
    for group in range(FF // 512):
        w_up = up[group]
        w_down = down[32 * group : 32 * group + 32].reshape(512, D)
        hidden = dot(normed, w_up) + ffb[group : group + 1, :]
        square = hidden * hidden
        tanh = jnp.tanh(c0 * (hidden + 0.044715 * (square * hidden)))
        half = 0.5 * (1.0 + tanh)
        active = (hidden * half).astype(BF)
        slope = half + hidden * (0.5 * c0) * (1.0 - tanh * tanh) * (1.0 + (3 * 0.044715) * square)
        part = dot(active, w_down)
        result = part if result is None else result + part
        grad_hidden = (slope * dot_nt(grads, w_down)).astype(BF)
        d_down[32 * group : 32 * group + 32] = dot_tn(active, grads).astype(BF).reshape(32, 16, D)
        d_up[group] = dot(normed_t, grad_hidden).astype(BF)
        ffg[group : group + 1, :] = row_sum(grad_hidden)
        part = dot_nt(grad_hidden, w_up)
        grad_normed = part if grad_normed is None else grad_normed + part
    done = copies_out(
        order,
        outs,
        lambda out, b, index: [
            (out.at[b, 0:4], d_up.at[:, rows16(index)]),
            (out.at[b, 4:8], d_down.at[down_rows(index)]),
        ],
        sems,
    )
    after_cross = x2[...]
    grad_out[...] = (after_cross + (result + vecs[9:10, :])).astype(BF)
    own, new = halves(grad_out, place, rows)
    out_keep[...], out_send[...] = own[...], new[...]
    part, d_gain, d_shift = norm_back(after_cross, vecs[12:13, :], grad_normed)
    grad_x2[...] = grads.astype(F32) + part
    small[...] = jnp.zeros_like(small)
    small[12:13, :] = d_gain
    small[8:9, :] = d_shift
    small[9:10, :] = row_sum(grads)
    wait_all(done)


def cross_back_kernel(n_pieces, n_outs, order, info, *refs):
    pieces = refs[:n_pieces]
    (x1, normed2, mem, cq, ck, cv, mixed2, log2, mask, grad_x2, vecs, small_in) = refs[n_pieces : n_pieces + 12]
    rest = refs[n_pieces + 12 :]
    (grad_x1, mem_keep, mem_send, small) = rest[:4]
    outs = rest[4 : 4 + n_outs]
    (weights, d_weights, grad_mixed, dq, dk, dv, grad_mem, sems) = rest[4 + n_outs :]
    place = info[0]
    wait = copies_in(
        order, pieces, lambda piece, b, index: [(piece.at[b, :, 2048:4096], weights.at[rows16(index)])], sems
    )
    small[...] = small_in[...]
    grad_y = grad_x2[...].astype(BF)
    d_weights[:, 1536:2048] = dot_tn(mixed2[...], grad_y).astype(BF)
    small[7:8, :] = row_sum(grad_y)
    wait_all(wait)
    grad_mixed[...] = dot_nt(grad_y, weights[:, 1536:2048]).astype(BF)
    attend_back(cq, ck, cv, mask[...] > 0, log2, grad_mixed, dq, dk, dv)
    memory = mem[...]
    memory_t = memory.T
    d_weights[:, 512:1024] = dot(memory_t, dk[...]).astype(BF)
    d_weights[:, 1024:1536] = dot(memory_t, dv[...]).astype(BF)
    d_weights[:, 0:512] = dot_tn(normed2[...], dq[...]).astype(BF)
    done = copies_out(
        order, outs, lambda out, b, index: [(out.at[b], d_weights.at[rows16(index)])], sems
    )
    small[6:7, :] = row_sum(dv[...])
    small[5:6, :] = row_sum(dq[...])
    grad_mem[...] = dot_nt(dk[...], weights[:, 512:1024]) + dot_nt(dv[...], weights[:, 1024:1536])
    own, new = halves(grad_mem, place, mem_keep.shape[0])
    mem_keep[...] = own[...]
    mem_send[...] = new[...].astype(BF)
    part, d_gain, d_shift = norm_back(x1[...], vecs[11:12, :], dot_nt(dq[...], weights[:, 0:512]))
    small[11:12, :] = d_gain
    small[4:5, :] = d_shift
    grad_x1[...] = grad_x2[...] + part
    wait_all(done)


def self_back_kernel(n_pieces, n_outs, order, info, *refs):
    pieces = refs[:n_pieces]
    (x0, normed1, q, k, v, mixed1, log1, grad_x1, vecs, small_in, ffg) = refs[n_pieces : n_pieces + 11]
    rest = refs[n_pieces + 11 :]
    (in_keep, in_send) = rest[:2]
    outs = rest[2 : 2 + n_outs]
    (weights, d_weights, d_small, small, grad_mixed, dq, dk, dv, grad_in, sems) = rest[2 + n_outs :]
    place, length = info[0], info[1]
    wait = copies_in(
        order, pieces, lambda piece, b, index: [(piece.at[b, :, 0:2048], weights.at[rows16(index)])], sems
    )
    small[...] = small_in[...]
    grad_y = grad_x1[...].astype(BF)
    d_weights[:, 1536:2048] = dot_tn(mixed1[...], grad_y).astype(BF)
    small[3:4, :] = row_sum(grad_y)
    wait_all(wait)
    grad_mixed[...] = dot_nt(grad_y, weights[:, 1536:2048]).astype(BF)
    rows = q.shape[0]
    attend_back(q, k, v, self_visible(length, rows), log1, grad_mixed, dq, dk, dv)
    normed_t = normed1[...].T
    for i, part in enumerate((dq, dk, dv)):
        d_weights[:, 512 * i : 512 * i + 512] = dot(normed_t, part[...]).astype(BF)
    small[1:2, :] = row_sum(dq[...])
    small[2:3, :] = row_sum(dv[...])
    grad_normed = (
        dot_nt(dq[...], weights[:, 0:512])
        + dot_nt(dk[...], weights[:, 512:1024])
        + dot_nt(dv[...], weights[:, 1024:1536])
    )
    part, d_gain, d_shift = norm_back(x0[...].astype(F32), vecs[10:11, :], grad_normed)
    small[10:11, :] = d_gain
    small[0:1, :] = d_shift
    for index in range(BLOCKS):
        tile = 128 * (index // 8)
        d_small[index] = small[:, tile : tile + 128].astype(BF)
        group, tile = index // 8, 128 * ((index // 2) % 4)
        d_small[index, 13:14, :] = ffg[group : group + 1, tile : tile + 128].astype(BF)
    done = copies_out(
        order,
        outs,
        lambda out, b, index: [
            (out.at[b, :, 0:2048], d_weights.at[rows16(index)]),
            (out.at[b, :, 2048:2176], d_small.at[index]),
        ],
        sems,
    )
    grad_in[...] = grad_x1[...] + part
    own, new = halves(grad_in, place, rows // 2)
    in_keep[...] = own[...]
    in_send[...] = new[...].astype(BF)
    wait_all(done)


VMEM = pl.BlockSpec(memory_space=pltpu.VMEM)
SMEM = pl.BlockSpec(memory_space=pltpu.SMEM)
ANY = pl.BlockSpec(memory_space=pl.ANY)


def shape(dims, dtype):
    return jax.ShapeDtypeStruct(dims, dtype)


def call(kernel, name, order, info, pieces, arrays, out_shapes, block_outs, scratch, flops):
    outs = [shape(*s) for s in out_shapes] + [shape(*s) for s in block_outs]
    moved = sum(a.size * a.dtype.itemsize for a in list(pieces) + list(arrays))
    return pl.pallas_call(
        kernel,
        name=name,
        out_shape=outs,
        in_specs=[SMEM, SMEM] + [ANY] * len(pieces) + [VMEM] * len(arrays),
        out_specs=[VMEM] * len(out_shapes) + [ANY] * len(block_outs),
        scratch_shapes=scratch,
        compiler_params=pltpu.CompilerParams(vmem_limit_bytes=50 * 1024 * 1024),
        cost_estimate=pl.CostEstimate(flops=flops, bytes_accessed=moved, transcendentals=0),
    )(order, info, *pieces, *arrays)


def flat_index(z, y, c, x):
    return ((z * 2 + y) * 2 + c) * 2 + x


def pairs_of(move):
    pairs = []
    for z in range(4):
        for y in range(2):
            for c in range(2):
                for x in range(2):
                    pairs.append((flat_index(z, y, c, x), flat_index(*move(z, y, c, x))))
    return pairs


CORE = pairs_of(lambda z, y, c, x: (z, y, 1 - c, x))
HOP_Z1 = pairs_of(lambda z, y, c, x: (z ^ 1 if c == 0 else z ^ 2, y, c, x))
HOP_Z2 = pairs_of(lambda z, y, c, x: (z ^ 2 if c == 0 else z ^ 1, y, c, x))
HOP_P1 = pairs_of(lambda z, y, c, x: (z, y, c, 1 - x) if c == 0 else (z, 1 - y, c, x))
HOP_P2 = pairs_of(lambda z, y, c, x: (z, y, c, 1 - x) if c == 1 else (z, 1 - y, c, x))
HOPS = (HOP_Z1, HOP_Z2, HOP_P1, HOP_P2)
FLIPS = ((8, 16, 1, 4), (16, 8, 4, 1))


def permute(value, pairs):
    return lax.ppermute(value, BOTH, pairs)


def join(*parts):
    return jnp.concatenate(parts, axis=0)


def block_order():
    me = lax.axis_index(BOTH)
    core = (me // 2) % 2
    k = jnp.arange(16, dtype=jnp.int32)
    planes = []
    for flips in FLIPS:
        planes.append(sum(((k >> b) & 1) * flip for b, flip in enumerate(flips)))
    own = jnp.where(core == 0, planes[0], planes[1])
    other = jnp.where(core == 0, planes[1], planes[0])
    return jnp.concatenate([me ^ own, (me ^ 2) ^ other]).astype(jnp.int32)


def gather(own):
    r1 = permute(own, HOPS[0])
    c2 = join(own, r1)
    r2 = permute(c2, HOPS[1])
    c4 = join(c2, r2)
    r3 = permute(c4, HOPS[2])
    c8 = join(c4, r3)
    r4 = permute(c8, HOPS[3])
    s8 = permute(c8, CORE)
    s4 = permute(r4, CORE)
    return [c8, r4, s8, s4]


def add(a, b):
    return (a.astype(F32) + b.astype(F32)).astype(BF)


def scatter(own, other):
    got = permute(other, CORE)
    for hop, count in ((3, 8), (2, 4), (1, 2)):
        send = add(own[count:], got[count:])
        keep = add(own[:count], got[:count])
        own, got = keep, permute(send, HOPS[hop])
    send = add(own[1:], got[1:])
    keep = own[0].astype(F32) + got[0].astype(F32)
    return keep + permute(send, HOPS[0])[0].astype(F32)


def small_rows(biases, gains, ffn_bias):
    count = biases.shape[0]
    columns = jnp.concatenate([biases, gains], axis=2).transpose(0, 2, 1)
    rows = jnp.tile(columns, (1, 1, 8))
    units = jnp.tile(ffn_bias.reshape(count, 1, 64), (1, 1, 2))
    return jnp.concatenate([rows, units, jnp.zeros((count, 2, 128), BF)], axis=1)


def pack_attention(qkv, out, cq, ckv, co, small):
    return jnp.concatenate([qkv, out, cq, ckv, co, small], axis=2)


def pack_ffn(up, down):
    count = up.shape[0]
    up = up.reshape(count, 16, 4, 512).transpose(0, 2, 1, 3)
    return jnp.concatenate([up, down.reshape(count, 4, 16, 512)], axis=1)


def per_device(n_devices, hidden_in, memory, lengths, source_mask, grad_out, *params):
    (w_qkv, w_out, w_cq, w_ckv, w_co, w_up, w_down, gains, biases, ffn_bias) = params
    permuted = n_devices == BLOCKS
    if not permuted:
        params = [lax.all_gather(p, BOTH, axis=0, tiled=True) for p in params]
        (w_qkv, w_out, w_cq, w_ckv, w_co, w_up, w_down, gains, biases, ffn_bias) = params
    count = w_qkv.shape[0] // 16
    cut = lambda w: w.reshape(count, -1, w.shape[1])
    attention = pack_attention(
        *(cut(w) for w in (w_qkv, w_out, w_cq, w_ckv, w_co)), small_rows(cut(biases), cut(gains), ffn_bias)
    )
    ffn = pack_ffn(cut(w_up), cut(w_down))

    place = lax.axis_index("seq")
    swap = lambda v: lax.ppermute(v, "seq", [(0, 1), (1, 0)])
    pick = lambda v, i: lax.dynamic_index_in_dim(v, i, 0, keepdims=False)
    rows, sources = hidden_in.shape[1], memory.shape[1]
    sent = jnp.concatenate([pick(hidden_in, 1 - place), pick(memory, 1 - place)], axis=0)
    new = swap(sent)
    h_own, m_own, g_own = (pick(v, place) for v in (hidden_in, memory, grad_out))
    h_new, m_new = new[:rows], new[rows:]
    g_new = swap(pick(grad_out, 1 - place))
    source = pick(source_mask, place)
    visible = ((source > 0) | (jnp.arange(source.shape[0]) == 0)).astype(F32)[:, None]
    info = jnp.stack([place, pick(lengths, place)]).astype(jnp.int32)

    if permuted:
        order = block_order()
        a_pieces, f_pieces = gather(attention), gather(ffn)
        halves_of = (16, 16)
    else:
        order = jnp.arange(BLOCKS, dtype=jnp.int32)
        a_pieces, f_pieces = [attention], [ffn]
        halves_of = (32,)

    tgt, src = 2 * rows, 2 * sources
    wide = (tgt, D)
    vec = ((16, D), F32)
    units = ((8, 512), F32)
    dma = pltpu.SemaphoreType.DMA
    mm = 2 * D * D
    (
        x0, mem, normed1, q, k, v, mixed1, log1, x1, normed2, cq, ck, cv, mixed2, log2, x2, normed3, vecs, ffb,
    ) = call(
        functools.partial(forward_kernel, len(a_pieces)), "forward", order, info, a_pieces,
        [h_own, h_new, m_own, m_new, visible],
        [
            (wide, BF), ((src, D), BF), (wide, BF), (wide, BF), (wide, BF), (wide, BF), (wide, BF),
            ((HEADS, tgt), F32), (wide, F32), (wide, BF), (wide, BF), ((src, D), BF), ((src, D), BF), (wide, BF),
            ((HEADS, tgt), F32), (wide, F32), (wide, BF), vec, units,
        ],
        [],
        [pltpu.VMEM((D, WIDE), BF), pltpu.VMEM((BLOCKS, 16, 128), BF), dma((BLOCKS,)), dma((BLOCKS,))],
        mm * (6 * tgt + 2 * src) * 2,
    )
    out_keep, out_send, grad_x2, small, ffg, *d_ffn = call(
        functools.partial(ffn_kernel, len(f_pieces), len(halves_of)), "ffn", order, info, f_pieces,
        [x2, normed3, g_own, g_new, vecs, ffb],
        [((rows, D), BF), ((rows, D), BF), (wide, F32), vec, units],
        [((n, 8, 16, 512), BF) for n in halves_of],
        [
            pltpu.VMEM((4, D, 512), BF), pltpu.VMEM((128, 16, D), BF), pltpu.VMEM((4, D, 512), BF),
            pltpu.VMEM((128, 16, D), BF), pltpu.VMEM(wide, BF), dma((2 * BLOCKS,)),
        ],
        mm * 24 * tgt,
    )
    grad_x1, mem_keep, mem_send, small, *d_cross = call(
        functools.partial(cross_back_kernel, len(a_pieces), len(halves_of)), "cross_back", order, info, a_pieces,
        [x1, normed2, mem, cq, ck, cv, mixed2, log2, visible, grad_x2, vecs, small],
        [(wide, F32), ((sources, D), F32), ((sources, D), BF), vec],
        [((n, 16, 2048), BF) for n in halves_of],
        [
            pltpu.VMEM((D, 2048), BF), pltpu.VMEM((D, 2048), BF), pltpu.VMEM(wide, BF), pltpu.VMEM(wide, BF),
            pltpu.VMEM((src, D), BF), pltpu.VMEM((src, D), BF), pltpu.VMEM((src, D), F32), dma((BLOCKS,)),
        ],
        mm * (8 * tgt + 4 * src),
    )
    in_keep, in_send, *d_self = call(
        functools.partial(self_back_kernel, len(a_pieces), len(halves_of)), "self_back", order, info, a_pieces,
        [x0, normed1, q, k, v, mixed1, log1, grad_x1, vecs, small, ffg],
        [((rows, D), F32), ((rows, D), BF)],
        [((n, 16, 2176), BF) for n in halves_of],
        [
            pltpu.VMEM((D, 2048), BF), pltpu.VMEM((D, 2048), BF), pltpu.VMEM((BLOCKS, 16, 128), BF),
            pltpu.VMEM((16, D), F32), pltpu.VMEM(wide, BF), pltpu.VMEM(wide, BF), pltpu.VMEM(wide, BF),
            pltpu.VMEM(wide, BF), pltpu.VMEM(wide, F32), dma((2 * BLOCKS,)),
        ],
        mm * 12 * tgt,
    )

    def both(keep, sent):
        got = swap(sent).astype(keep.dtype)
        return jnp.where(place == 0, jnp.stack([keep, got]), jnp.stack([got, keep]))

    outputs = (both(out_keep, out_send), both(in_keep, in_send), both(mem_keep, mem_send))

    if permuted:
        g_ffn, g_cross, g_self = scatter(*d_ffn), scatter(*d_cross), scatter(*d_self)
        me = lax.axis_index(BOTH)
        g_small = g_self[:, 2048:]
        columns = lax.dynamic_slice(g_small, (0, (me % 8) * 16), (13, 16)).T
        g_unit = lax.dynamic_slice(g_small, (13, (me % 2) * 64), (1, 64)).reshape(64)
        g_up = g_ffn[:4].transpose(1, 0, 2).reshape(16, FF)
        g_down = g_ffn[4:].reshape(64, D)
        rest = (
            g_self[:, :1536], g_self[:, 1536:2048], g_cross[:, :512], g_cross[:, 512:1536], g_cross[:, 1536:],
            g_up, g_down, columns[:, 10:], columns[:, :10], g_unit,
        )
    else:
        d_ffn, d_cross, d_self = (d[0].astype(F32) for d in (d_ffn, d_cross, d_self))
        d_small = d_self[:, :, 2048:]
        columns = jnp.concatenate([d_small[i, :13, 16 * (i % 8) : 16 * (i % 8) + 16].T for i in range(BLOCKS)])
        d_unit = jnp.concatenate([d_small[i, 13, 64 * (i % 2) : 64 * (i % 2) + 64] for i in range(BLOCKS)])
        d_self = d_self[:, :, :2048].reshape(D, 2048)
        d_cross = d_cross.reshape(D, 2048)
        d_up = d_ffn[:, :4].transpose(0, 2, 1, 3).reshape(D, FF)
        d_down = d_ffn[:, 4:].reshape(FF, D)
        rest = tuple(
            lax.psum_scatter(d, BOTH, scatter_dimension=0, tiled=True)
            for d in (
                d_self[:, :1536], d_self[:, 1536:], d_cross[:, :512], d_cross[:, 512:1536], d_cross[:, 1536:],
                d_up, d_down, columns[:, 10:], columns[:, :10], d_unit,
            )
        )
    return outputs + rest


def solution(mesh):
    rows = P(BOTH, None)
    part = P("batch", "seq", None)
    return jax.shard_map(
        functools.partial(per_device, mesh.devices.size),
        mesh=mesh,
        in_specs=(part, part, P("batch"), P("batch", None), part) + (rows,) * 9 + (P(BOTH),),
        out_specs=(part, part, part) + (rows,) * 9 + (P(BOTH),),
        check_vma=False,
    )
```

```python
import functools

import jax
import jax.numpy as jnp
from jax import lax
from jax.experimental import pallas as pl
from jax.experimental.pallas import tpu as pltpu
from jax.sharding import PartitionSpec as P

D = 512
FF = 2048
HEADS = 8
HEAD_DIM = 64
EPSILON = 1e-05
NEGATIVE = -1000000000.0
SCALE = HEAD_DIM ** (-0.5)
BLOCKS = 32
WIDE = 4096
BF = jnp.bfloat16
F32 = jnp.float32
BOTH = ("batch", "seq")

QKV, OUT, CQ, CKV, CO = (0, 1536), (1536, 2048), (2048, 2560), (2560, 3584), (3584, 4096)


def dot(a, b):
    return lax.dot_general(a, b, (((1,), (0,)), ((), ())), preferred_element_type=F32)


def dot_nt(a, b):
    return lax.dot_general(a, b, (((1,), (1,)), ((), ())), preferred_element_type=F32)


def dot_tn(a, b):
    return lax.dot_general(a, b, (((0,), (0,)), ((), ())), preferred_element_type=F32)


def norm(values):
    centred = values - jnp.mean(values, axis=-1, keepdims=True)
    rate = lax.rsqrt(jnp.mean(centred * centred, axis=-1, keepdims=True) + EPSILON)
    return centred * rate, rate


def norm_back(values, gain, grad):
    unit, rate = norm(values)
    scaled = grad * gain
    part = rate * (
        scaled
        - jnp.mean(scaled, axis=-1, keepdims=True)
        - unit * jnp.mean(scaled * unit, axis=-1, keepdims=True)
    )
    return part, row_sum(grad * unit), row_sum(grad)


def row_sum(values):
    return jnp.sum(values.astype(F32), axis=0, keepdims=True)


def lane_masks(dtype):
    lane = lax.broadcasted_iota(jnp.int32, (1, 128), 1)
    return [(lane // HEAD_DIM == j).astype(dtype) for j in range(2)]


def scores_t(keys, queries, visible):
    return jnp.where(visible, dot_nt(keys, queries) * SCALE, NEGATIVE)


def attend(q_ref, k_ref, v_ref, visible, mixed_ref, log_ref):
    masks = lane_masks(BF)
    for pair in range(HEADS // 2):
        cols = slice(128 * pair, 128 * pair + 128)
        queries, keys, values = q_ref[:, cols], k_ref[:, cols], v_ref[:, cols]
        total = None
        for j in range(2):
            scores = scores_t(keys, queries * masks[j], visible)
            top = jnp.max(scores, axis=0, keepdims=True)
            exponent = jnp.exp(scores - top)
            row_total = jnp.sum(exponent, axis=0, keepdims=True)
            probs = (exponent * (1.0 / row_total)).astype(BF)
            log_ref[2 * pair + j : 2 * pair + j + 1, :] = top + jnp.log(row_total)
            part = dot_tn(probs, values * masks[j])
            total = part if total is None else total + part
        mixed_ref[:, cols] = total.astype(BF)


def attend_back(q_ref, k_ref, v_ref, visible, log_ref, grad_ref, dq_ref, dk_ref, dv_ref):
    masks = lane_masks(BF)
    for pair in range(HEADS // 2):
        cols = slice(128 * pair, 128 * pair + 128)
        queries, keys, values, grads = q_ref[:, cols], k_ref[:, cols], v_ref[:, cols], grad_ref[:, cols]
        dq = dk = dv = None
        for j in range(2):
            own_q, own_k, own_g = queries * masks[j], keys * masks[j], grads * masks[j]
            scores = scores_t(keys, own_q, visible)
            probs = jnp.exp(scores - log_ref[2 * pair + j : 2 * pair + j + 1, :])
            grad_probs = dot_nt(values, own_g)
            part_v = dot(probs.astype(BF), own_g)
            inner = jnp.sum(probs * grad_probs, axis=0, keepdims=True)
            low = (probs * (grad_probs - inner)).astype(BF)
            part_k = dot(low, own_q)
            part_q = dot_tn(low, own_k)
            dq = part_q if dq is None else dq + part_q
            dk = part_k if dk is None else dk + part_k
            dv = part_v if dv is None else dv + part_v
        dq_ref[:, cols] = (dq * SCALE).astype(BF)
        dk_ref[:, cols] = (dk * SCALE).astype(BF)
        dv_ref[:, cols] = dv.astype(BF)


def place_blocks(order, base, pieces, put):
    for i, piece in enumerate(pieces):
        if piece is None:
            continue
        count = piece.shape[0]

        @pl.loop(0, count)
        def _(b, piece=piece, first=base + i * count):
            put(piece, b, order[first + b])


def rows16(index):
    return pl.ds(pl.multiple_of(index * 16, 16), 16)


def halves(ref, place, rows):
    own = pl.ds(pl.multiple_of(place * rows, rows), rows)
    other = pl.ds(pl.multiple_of((1 - place) * rows, rows), rows)
    return ref.at[own], ref.at[other]


def self_visible(length, rows):
    key = lax.broadcasted_iota(jnp.int32, (rows, rows), 0)
    query = lax.broadcasted_iota(jnp.int32, (rows, rows), 1)
    return (key <= query) & (key < length)


def cross_visible(mask):
    row = jnp.broadcast_to(mask[...].astype(F32), (8, mask.shape[1]))
    column = row.T[:, 0:1]
    return (column > 0) | (lax.broadcasted_iota(jnp.int32, column.shape, 0) == 0)


def pack_kernel(
    me, all_lengths, all_units, gains, biases, qkv, out, cq, ckv, co, up, down, hidden, memory, grads, masks,
    order, info, attention, w_up, w_down, sent, kept, mask, token, rows, gain_rows, bias_rows, lengths, units, sems,
):
    index = me[0]
    core = (index // 2) % 2
    place = index % 2
    far = 1 - place
    moves = [(gains, gain_rows), (biases, bias_rows), (masks.at[pl.ds(place, 1)], mask), (up, w_up), (down, w_down)]
    moves += [(all_lengths, lengths), (all_units, units)]
    first = 0
    for part in (hidden, memory, grads):
        last = first + part.shape[1]
        moves.append((part.at[far], sent.at[first:last]))
        moves.append((part.at[place], kept.at[first:last]))
        first = last
    first = 0
    for part in (qkv, out, cq, ckv, co):
        width = part.shape[1]
        moves.append((part, attention.at[0, :, first : first + width]))
        first += width
    moves = [pltpu.make_async_copy(a, b, sems.at[i]) for i, (a, b) in enumerate(moves)]
    for move in moves:
        move.start()
    info[0] = place
    for kind, both in enumerate(FLIPS):
        for k in range(16):
            plane = [sum(((k >> b) & 1) * flip for b, flip in enumerate(flips)) for flips in both]
            order[BLOCKS * kind + k] = index ^ jnp.where(core == 0, plane[0], plane[1])
            order[BLOCKS * kind + 16 + k] = index ^ jnp.where(core == 0, plane[1] | 2, plane[0] | 2)
    token[...] = jnp.zeros_like(token)
    rows[...] = jnp.zeros_like(rows)
    lane = lax.broadcasted_iota(jnp.int32, (16, 128), 1)
    spread = (lane % 16 == lax.broadcasted_iota(jnp.int32, (16, 128), 0)).astype(BF)
    unit_lane = lax.broadcasted_iota(jnp.int32, (64, 128), 1)
    unit_spread = (unit_lane % 64 == lax.broadcasted_iota(jnp.int32, (64, 128), 0)).astype(BF)
    for move in moves:
        move.wait()
    info[1] = lengths[place]
    rows[13:14, :] = dot(jnp.broadcast_to(units[...], (16, 64)), unit_spread)[0:1, :]
    rows[0:10, :] = dot_tn(bias_rows[...], spread)
    rows[10:13, :] = dot(gain_rows[...], spread)
    attention[0, :, WIDE : WIDE + 128] = rows[...].astype(BF)


def join_kernel(have, got, extra, joined):
    count = have.shape[0]
    joined[0:count] = have[...]
    joined[count:] = got[...]


def pass_kernel(value, out):
    out[...] = value[...]


def add_kernel(own, got, send, keep):
    count = send.shape[0]
    send[...] = (own[count:].astype(F32) + got[count:].astype(F32)).astype(send.dtype)
    keep[...] = (own[:count].astype(F32) + got[:count].astype(F32)).astype(keep.dtype)


def last_kernel(own, got, out):
    out[...] = own[0] + got[0].astype(F32)


def last_cross_kernel(own, got, d_cq, d_ckv, d_co, d_out):
    total = own[0] + got[0].astype(F32)
    d_cq[...] = total[:, 0:512]
    d_ckv[...] = total[:, 512:1536]
    d_co[...] = total[:, 1536:2048]
    d_out[...] = total[:, 2048:2560]


def last_self_kernel(me, own, got, d_qkv, d_gains, d_biases, d_units):
    total = own[0] + got[0].astype(F32)
    d_qkv[...] = total[:, 0:1536]
    small = total[:, 1536:1664]
    index = me[0]
    vectors = pltpu.roll(small, (128 - 16 * (index % 8)) % 128, 1)[:, 0:16]
    d_gains[...] = vectors[10:13, :]
    d_biases[...] = vectors.T[:, 0:10]
    d_units[...] = pltpu.roll(small, (128 - 64 * (index % 2)) % 128, 1)[13:14, 0:64]


def halves_kernel(info, kept, got, out):
    place = info[0]
    out[place] = kept[...]
    out[1 - place] = got[...].astype(out.dtype)


def self_forward_kernel(
    base, order, info, p0, p1, p2, p3, kept, new, weights, vecs, ffb, x0, normed1, q, k, v, mixed1, log1, x1, normed2,
    small,
):
    place, length = info[0], info[1]

    def put(piece, b, index):
        weights[rows16(index), :] = piece[b, :, 0:2048]
        small[index] = piece[b, :, WIDE : WIDE + 128]

    place_blocks(order, base, (p0, p1, p2, p3), put)
    rows = x0.shape[0] // 2
    own, other = halves(x0, place, rows)
    own[...], other[...] = kept[0:rows], new[0:rows]
    hidden = x0[...].astype(F32)
    lane = lax.broadcasted_iota(jnp.int32, (16, 128), 1)
    for tile in range(D // 128):
        row = jnp.zeros((16, 128), F32)
        for i in range(8):
            row = jnp.where(lane // 16 == i, small[8 * tile + i].astype(F32), row)
        vecs[:, 128 * tile : 128 * tile + 128] = row
    ffb[...] = jnp.zeros_like(ffb)
    for tile in range(FF // 128):
        row = jnp.where(lane < 64, small[2 * tile].astype(F32), small[2 * tile + 1].astype(F32))
        ffb[tile // 4 : tile // 4 + 1, 128 * (tile % 4) : 128 * (tile % 4) + 128] = row[13:14, :]

    def bias(j):
        return vecs[j : j + 1, :]

    normed1[...] = (norm(hidden)[0] * bias(10) + bias(0)).astype(BF)
    q[...] = (dot(normed1[...], weights[:, 0:512]) + bias(1)).astype(BF)
    k[...] = dot(normed1[...], weights[:, 512:1024]).astype(BF)
    v[...] = (dot(normed1[...], weights[:, 1024:1536]) + bias(2)).astype(BF)
    attend(q, k, v, self_visible(length, 2 * rows), mixed1, log1)
    after_self = hidden + (dot(mixed1[...], weights[:, 1536:2048]) + bias(3))
    x1[...] = after_self
    normed2[...] = (norm(after_self)[0] * bias(11) + bias(4)).astype(BF)


def cross_forward_kernel(
    base, order, info, p0, p1, p2, p3, kept, new, mask, vecs, x1, normed2,
    weights, mem, cq, ck, cv, mixed2, log2, x2, normed3,
):
    place = info[0]

    def put(piece, b, index):
        weights[rows16(index), :] = piece[b, :, 2048:4096]

    place_blocks(order, base, (p0, p1, p2, p3), put)
    sources = mem.shape[0] // 2
    first = x1.shape[0] // 2
    own, other = halves(mem, place, sources)
    own[...], other[...] = kept[first : first + sources], new[first : first + sources]

    def bias(j):
        return vecs[j : j + 1, :]

    ck[...] = dot(mem[...], weights[:, 512:1024]).astype(BF)
    cv[...] = (dot(mem[...], weights[:, 1024:1536]) + bias(6)).astype(BF)
    cq[...] = (dot(normed2[...], weights[:, 0:512]) + bias(5)).astype(BF)
    attend(cq, ck, cv, cross_visible(mask), mixed2, log2)
    after_cross = x1[...] + (dot(mixed2[...], weights[:, 1536:2048]) + bias(7))
    x2[...] = after_cross
    normed3[...] = (norm(after_cross)[0] * bias(12) + bias(8)).astype(BF)


def four_rows(index):
    return pl.ds(pl.multiple_of(index * 4, 4), 4)


def ffn_kernel(
    bases, order, info, u0, u1, u2, u3, w0, w1, w2, w3, x2, normed3, kept, new, vecs, ffb,
    out_keep, out_send, up, grad_hidden, grad_out, own_out, other_out,
    down, d_down, result,
):
    place = info[0]

    def put_up(piece, b, index):
        up[rows16(index), :] = piece[b]

    def put_down(piece, b, index):
        down[four_rows(index)] = piece[b]

    place_blocks(order, bases[0], (u0, u1, u2, u3), put_up)
    place_blocks(order, bases[1], (w0, w1, w2, w3), put_down)
    rows = out_keep.shape[0]
    first = kept.shape[0] - rows
    own, other = halves(grad_out, place, rows)
    own[...], other[...] = kept[first:], new[first:]
    grads = grad_out[...]
    normed = normed3[...]
    total = None
    c0 = (2.0 / jnp.pi) ** 0.5
    for group in range(FF // 512):
        w_down = down[32 * group : 32 * group + 32].reshape(512, D)
        hidden = dot(normed, up[:, 512 * group : 512 * group + 512]) + ffb[group : group + 1, :]
        square = hidden * hidden
        tanh = jnp.tanh(c0 * (hidden + 0.044715 * (square * hidden)))
        half = 0.5 * (1.0 + tanh)
        active = (hidden * half).astype(BF)
        slope = half + hidden * (0.5 * c0) * (1.0 - tanh * tanh) * (1.0 + (3 * 0.044715) * square)
        part = dot(active, w_down)
        total = part if total is None else total + part
        grad_hidden[:, 512 * group : 512 * group + 512] = (slope * dot_nt(grads, w_down)).astype(BF)
        d_down[32 * group : 32 * group + 32] = dot_tn(active, grads).astype(BF).reshape(32, 16, D)
    take_blocks(order, bases[2], (own_out, other_out), lambda index: d_down[four_rows(index)])
    result[...] = (x2[...] + (total + vecs[9:10, :])).astype(BF)
    own, other = halves(result, place, rows)
    out_keep[...], out_send[...] = own[...], other[...]


def ffn_back_kernel(
    base, order, info, up, grad_hidden, grad_out, x2, normed3, vecs, grad_x2, small, ffg, own_out, other_out, d_up
):
    normed_t = normed3[...].T
    grad_normed = None
    ffg[...] = jnp.zeros_like(ffg)
    for group in range(FF // 512):
        grad = grad_hidden[:, 512 * group : 512 * group + 512]
        d_up[:, 512 * group : 512 * group + 512] = dot(normed_t, grad).astype(BF)
        ffg[group : group + 1, :] = row_sum(grad)
        part = dot_nt(grad, up[:, 512 * group : 512 * group + 512])
        grad_normed = part if grad_normed is None else grad_normed + part
    take_blocks(order, base, (own_out, other_out), lambda index: d_up[rows16(index), :])
    part, d_gain, d_shift = norm_back(x2[...], vecs[12:13, :], grad_normed)
    grads = grad_out[...]
    grad_x2[...] = grads.astype(F32) + part
    small[...] = jnp.zeros_like(small)
    small[12:13, :] = d_gain
    small[8:9, :] = d_shift
    small[9:10, :] = row_sum(grads)


def cross_back_kernel(
    base, order, info, weights, weights1, x1, normed2, mem, cq, ck, cv, mixed1, mixed2, log2, mask, grad_x2, vecs, small_in,
    grad_x1, grad_mixed1, mem_keep, mem_send, small, own_out, other_out,
    d_weights, grad_mixed, dq, dk, dv, grad_mem,
):
    place = info[0]
    small[...] = small_in[...]
    grad_y = grad_x2[...].astype(BF)
    d_weights[:, 1536:2048] = dot_tn(mixed2[...], grad_y).astype(BF)
    small[7:8, :] = row_sum(grad_y)
    grad_mixed[...] = dot_nt(grad_y, weights[:, 1536:2048]).astype(BF)
    attend_back(cq, ck, cv, cross_visible(mask), log2, grad_mixed, dq, dk, dv)
    memory_t = mem[...].T
    d_weights[:, 512:1024] = dot(memory_t, dk[...]).astype(BF)
    d_weights[:, 1024:1536] = dot(memory_t, dv[...]).astype(BF)
    d_weights[:, 0:512] = dot_tn(normed2[...], dq[...]).astype(BF)
    small[6:7, :] = row_sum(dv[...])
    small[5:6, :] = row_sum(dq[...])
    grad_mem[...] = dot_nt(dk[...], weights[:, 512:1024]) + dot_nt(dv[...], weights[:, 1024:1536])
    own, other = halves(grad_mem, place, mem_keep.shape[0])
    mem_keep[...] = own[...]
    mem_send[...] = other[...].astype(BF)
    part, d_gain, d_shift = norm_back(x1[...], vecs[11:12, :], dot_nt(dq[...], weights[:, 0:512]))
    small[11:12, :] = d_gain
    small[4:5, :] = d_shift
    total = grad_x2[...] + part
    grad_x1[...] = total
    grad_y = total.astype(BF)
    d_weights[:, 2048:2560] = dot_tn(mixed1[...], grad_y).astype(BF)
    small[3:4, :] = row_sum(grad_y)
    grad_mixed1[...] = dot_nt(grad_y, weights1[:, 1536:2048]).astype(BF)
    take_blocks(order, base, (own_out, other_out), lambda index: d_weights[rows16(index), :])


def self_back_kernel(
    base, order, info, weights, x0, normed1, q, k, v, log1, grad_x1, grad_mixed, vecs, small_in, ffg,
    in_keep, in_send, own_out, other_out,
    d_weights, d_small, small, dq, dk, dv, grad_in,
):
    place, length = info[0], info[1]
    small[...] = small_in[...]
    rows = q.shape[0]
    attend_back(q, k, v, self_visible(length, rows), log1, grad_mixed, dq, dk, dv)
    normed_t = normed1[...].T
    for i, part in enumerate((dq, dk, dv)):
        d_weights[:, 512 * i : 512 * i + 512] = dot(normed_t, part[...]).astype(BF)
    small[1:2, :] = row_sum(dq[...])
    small[2:3, :] = row_sum(dv[...])
    grad_normed = (
        dot_nt(dq[...], weights[:, 0:512])
        + dot_nt(dk[...], weights[:, 512:1024])
        + dot_nt(dv[...], weights[:, 1024:1536])
    )
    part, d_gain, d_shift = norm_back(x0[...].astype(F32), vecs[10:11, :], grad_normed)
    small[10:11, :] = d_gain
    small[0:1, :] = d_shift
    for index in range(BLOCKS):
        tile = 128 * (index // 8)
        d_small[index] = small[:, tile : tile + 128].astype(BF)
        group, tile = index // 8, 128 * ((index // 2) % 4)
        d_small[index, 13:14, :] = ffg[group : group + 1, tile : tile + 128].astype(BF)
    first = base
    for out in (own_out, other_out):
        if out is None:
            continue

        @pl.loop(0, out.shape[0])
        def _(b, out=out, first=first):
            index = order[first + b]
            out[b, :, 0:1536] = d_weights[rows16(index), :]
            out[b, :, 1536:1664] = d_small[index]

        first += out.shape[0]
    grad_in[...] = grad_x1[...] + part
    own, other = halves(grad_in, place, rows // 2)
    in_keep[...] = own[...]
    in_send[...] = other[...].astype(BF)


def take_blocks(order, base, outs, take):
    first = base
    for out in outs:
        if out is None:
            continue

        @pl.loop(0, out.shape[0])
        def _(b, out=out, first=first):
            out[b] = take(order[first + b])

        first += out.shape[0]


VMEM = pl.BlockSpec(memory_space=pltpu.VMEM)
SMEM = pl.BlockSpec(memory_space=pltpu.SMEM)
HBM = pl.BlockSpec(memory_space=pltpu.HBM)


def shape(dims, dtype):
    return jax.ShapeDtypeStruct(dims, dtype)


EVENT = 1_000_000_000


class Line:
    def __init__(self):
        self.token = None

    def call(self, kernel, name, inputs, outs, scratch=(), scalars=0, flops=1):
        given = [i for i in inputs if i is not None]
        made = [o for o in outs if o is not None]
        tokens = [self.token] if self.token is not None else []

        def body(*refs):
            refs = list(refs)
            taken = [None if i is None else refs.pop(0) for i in inputs]
            for _ in tokens:
                refs.pop(0)
            given_out = [None if o is None else refs.pop(0) for o in outs]
            out_token = refs.pop(0)
            out_token[...] = jnp.zeros_like(out_token)
            kernel(*taken, *given_out, *refs)

        moved = sum(a.size * a.dtype.itemsize for a in given)
        *results, self.token = pl.pallas_call(
            body,
            name=name,
            out_shape=[shape(*o) for o in made] + [shape((8, 128), F32)],
            in_specs=[SMEM] * scalars + [VMEM] * (len(given) - scalars + len(tokens)),
            out_specs=[VMEM] * (len(made) + 1),
            scratch_shapes=list(scratch),
            compiler_params=pltpu.CompilerParams(vmem_limit_bytes=32 * 1024 * 1024),
            cost_estimate=pl.CostEstimate(flops=flops, bytes_accessed=1, transcendentals=0),
        )(*given, *tokens)
        results = iter(results)
        return [None if o is None else next(results) for o in outs]


def flat_index(z, y, c, x):
    return ((z * 2 + y) * 2 + c) * 2 + x


def pairs_of(move):
    pairs = []
    for z in range(4):
        for y in range(2):
            for c in range(2):
                for x in range(2):
                    pairs.append((flat_index(z, y, c, x), flat_index(*move(z, y, c, x))))
    return pairs


CORE = pairs_of(lambda z, y, c, x: (z, y, 1 - c, x))
SIDE = pairs_of(lambda z, y, c, x: (z, y, c, 1 - x))
HOP_Z1 = pairs_of(lambda z, y, c, x: (z ^ 1 if c == 0 else z ^ 2, y, c, x))
HOP_Z2 = pairs_of(lambda z, y, c, x: (z ^ 2 if c == 0 else z ^ 1, y, c, x))
HOP_P1 = pairs_of(lambda z, y, c, x: (z, y, c, 1 - x) if c == 0 else (z, 1 - y, c, x))
HOP_P2 = pairs_of(lambda z, y, c, x: (z, y, c, 1 - x) if c == 1 else (z, 1 - y, c, x))
HOPS = (
    (HOP_Z1, HOP_Z2, HOP_P1, HOP_P2),
    (HOP_P1, HOP_P2, HOP_Z1, HOP_Z2),
    (HOP_P1, HOP_Z1, HOP_Z2, HOP_P2),
)
FLIPS = (
    ((8, 16, 1, 4), (16, 8, 4, 1)),
    ((1, 4, 8, 16), (4, 1, 16, 8)),
    ((1, 8, 16, 4), (4, 16, 8, 1)),
)
GATHER_KIND = dict(a=0, u=0, w=1)
GATHER = "a:12 w:12 u:12 a:12 w:12 u:12 a:12 w:12 u:12"
SCATTER_KIND = dict(d=2, u=2, c=0, s=0)
SCATTER = (
    "d:0 u:0 X:0 Y:0 d:12 s:3 u:0 c:0 d:0.3 o:4 s:0.6 c:0 u:0 s:0.3 d:1.5"
    " c:0 u:0 d:0.6 s:1.5 u:0 c:0 h:0 s:1 m:0 c:0"
)


def plan(text):
    return [(item.split(":")[0], int(float(item.split(":")[1]) * EVENT) + 1) for item in text.split()]


def permute(value, pairs):
    return lax.ppermute(value, BOTH, pairs)


class Gather:
    def __init__(self, line, name, own):
        self.line, self.name, self.have, self.hop = line, name, own, 0
        self.hops = HOPS[GATHER_KIND[name]]

    def start(self):
        with jax.named_scope(f"gather_{self.name}_hop{self.hop}"):
            self.coming = permute(self.have, self.hops[self.hop])
        self.hop += 1
        if self.hop == 4:
            with jax.named_scope(f"gather_{self.name}_core0"):
                self.core = permute(self.have, CORE)

    def step(self, extra, cost):
        dims = self.have.shape
        (self.have,) = self.line.call(
            join_kernel, f"join_{self.name}{self.hop}", [self.have, self.coming, extra],
            [((2 * dims[0],) + dims[1:], BF)], flops=cost,
        )
        self.start()

    def finish(self, tied=False):
        if tied:
            (self.coming,) = self.line.call(
                pass_kernel, f"pass_{self.name}", [self.coming], [(self.coming.shape, BF)], flops=12 * EVENT
            )
        with jax.named_scope(f"gather_{self.name}_core1"):
            return [self.have, self.coming, self.core, permute(self.coming, CORE)]


class Scatter:
    def __init__(self, line, name, own, other):
        self.line, self.name, self.own, self.hop = line, name, own, 4
        self.hops = HOPS[SCATTER_KIND[name]]
        with jax.named_scope(f"scatter_{name}_core"):
            self.coming = permute(other, CORE)

    def step(self, cost):
        self.hop -= 1
        dims = (1 << self.hop,) + self.own.shape[1:]
        send, self.own = self.line.call(
            add_kernel, f"add_{self.name}{self.hop}", [self.own, self.coming],
            [(dims, BF), (dims, BF if self.hop else F32)], flops=cost,
        )
        with jax.named_scope(f"scatter_{self.name}_hop{self.hop}"):
            self.coming = permute(send, self.hops[self.hop])


def small_rows(biases, gains, ffn_bias):
    count = biases.shape[0]
    columns = jnp.concatenate([biases, gains], axis=2).transpose(0, 2, 1)
    rows = jnp.tile(columns, (1, 1, 8))
    units = jnp.tile(ffn_bias.reshape(count, 1, 64), (1, 1, 2))
    return jnp.concatenate([rows, units, jnp.zeros((count, 2, 128), BF)], axis=1)


def pack_attention(qkv, out, cq, ckv, co, small):
    return jnp.concatenate([qkv, out, cq, ckv, co, small], axis=2)


def packed(hidden_in, memory, lengths, source_mask, grad_out, params, me):
    (w_qkv, w_out, w_cq, w_ckv, w_co, w_up, w_down, gains, biases, ffn_bias) = params
    rows = 2 * hidden_in.shape[1] + memory.shape[1]
    return pl.pallas_call(
        pack_kernel,
        name="pack",
        out_shape=[
            shape((len(FLIPS) * BLOCKS,), jnp.int32), shape((2,), jnp.int32), shape((1, 16, WIDE + 128), BF),
            shape((16, FF), BF), shape((64, D), BF), shape((rows, D), BF), shape((rows, D), BF),
            shape((1, source_mask.shape[1]), jnp.int32), shape((8, 128), F32),
        ],
        in_specs=[SMEM] + [HBM] * 15,
        out_specs=[SMEM, SMEM] + [VMEM] * 7,
        scratch_shapes=[
            pltpu.VMEM((16, 128), F32), pltpu.VMEM((3, 16), BF), pltpu.VMEM((16, 10), BF),
            pltpu.SMEM(lengths.shape, jnp.int32), pltpu.VMEM((1, 64), BF), pltpu.SemaphoreType.DMA((18,)),
        ],
        compiler_params=pltpu.CompilerParams(vmem_limit_bytes=16 * 1024 * 1024),
    )(
        me,
        *(
            pltpu.with_memory_space_constraint(v, pltpu.HBM)
            for v in (
                lengths, ffn_bias.reshape(1, 64), gains.T, biases, w_qkv, w_out, w_cq, w_ckv, w_co, w_up, w_down, hidden_in, memory, grad_out, source_mask,
            )
        ),
    )


def per_device(n_devices, hidden_in, memory, lengths, source_mask, grad_out, *params):
    permuted = n_devices == BLOCKS
    rows, sources = hidden_in.shape[1], memory.shape[1]
    tgt, src = 2 * rows, 2 * sources
    line = Line()

    def swap(value, name):
        with jax.named_scope(f"swap_{name}"):
            return lax.ppermute(value, "seq", [(0, 1), (1, 0)])

    place = lax.axis_index("seq")
    if permuted:
        me = lax.axis_index(BOTH).astype(jnp.int32).reshape(1)
        order, info, attention, w_up, w_down, sent, kept, mask, line.token = packed(
            hidden_in, memory, lengths, source_mask, grad_out, params, me
        )
        chunks = dict(
            a=Gather(line, "a", attention), w=Gather(line, "w", w_down.reshape(1, 4, 16, D)),
            u=Gather(line, "u", w_up[None]),
        )
        chunks["a"].start()
        chunks["w"].start()
        new = swap(sent, "in")
        chunks["u"].start()
        for name, cost in plan(GATHER):
            chunks[name].step(new if name == "a" and chunks[name].hop == 2 else None, cost)
        a_pieces = chunks["a"].finish()
        halves_of = (16, 16)
        base = lambda kind: BLOCKS * kind
    else:
        params = [lax.all_gather(p, BOTH, axis=0, tiled=True) for p in params]
        (w_qkv, w_out, w_cq, w_ckv, w_co, w_up, w_down, gains, biases, ffn_bias) = params
        cut = lambda w: w.reshape(BLOCKS, -1, w.shape[1])
        attention = pack_attention(
            *(cut(w) for w in (w_qkv, w_out, w_cq, w_ckv, w_co)), small_rows(cut(biases), cut(gains), ffn_bias)
        )
        pick = lambda v, i: lax.dynamic_index_in_dim(v, i, 0, keepdims=False)
        both_of = lambda i: jnp.concatenate([pick(v, i) for v in (hidden_in, memory, grad_out)], axis=0)
        kept, new = both_of(place), swap(both_of(1 - place), "in")
        mask = pick(source_mask, place)[None]
        info = jnp.stack([place, pick(lengths, place)]).astype(jnp.int32)
        order = jnp.arange(BLOCKS, dtype=jnp.int32)
        a_pieces = [attention, None, None, None]
        halves_of = (BLOCKS, None)
        base = lambda kind: 0

    wide = (tgt, D)
    vec = ((16, D), F32)
    units = ((8, 512), F32)
    blocks = lambda *dims: [None if n is None else ((n,) + dims, BF) for n in halves_of]
    weights1, vecs, ffb, x0, normed1, q, k, v, mixed1, log1, x1, normed2 = line.call(
        functools.partial(self_forward_kernel, base(GATHER_KIND["a"])), "self_forward", [order, info, *a_pieces, kept, new],
        [
            ((D, 2048), BF), vec, units, (wide, BF), (wide, BF), (wide, BF), (wide, BF), (wide, BF), (wide, BF),
            ((HEADS, tgt), F32), (wide, F32), (wide, BF),
        ],
        [pltpu.VMEM((BLOCKS, 16, 128), BF)], 2,
    )
    weights2, mem, cq, ck, cv, mixed2, log2, x2, normed3 = line.call(
        functools.partial(cross_forward_kernel, base(GATHER_KIND["a"])), "cross_forward",
        [order, info, *a_pieces, kept, new, mask, vecs, x1, normed2],
        [
            ((D, 2048), BF), ((src, D), BF), (wide, BF), ((src, D), BF), ((src, D), BF), (wide, BF),
            ((HEADS, tgt), F32), (wide, F32), (wide, BF),
        ],
        [], 2,
    )
    if permuted:
        w_pieces, u_pieces = chunks["w"].finish(True), chunks["u"].finish(True)
    else:
        u_pieces, w_pieces = [cut(w_up), None, None, None], [w_down.reshape(BLOCKS, 4, 16, D), None, None, None]
    bases = (base(GATHER_KIND["u"]), base(GATHER_KIND["w"]), base(SCATTER_KIND["d"]))
    out_keep, out_send, up, grad_hidden, g_full, *d_down = line.call(
        functools.partial(ffn_kernel, bases), "ffn",
        [order, info, *u_pieces, *w_pieces, x2, normed3, kept, new, vecs, ffb],
        [((rows, D), BF), ((rows, D), BF), ((D, FF), BF), ((tgt, FF), BF), (wide, BF), *blocks(4, 16, D)],
        [pltpu.VMEM((128, 16, D), BF), pltpu.VMEM((128, 16, D), BF), pltpu.VMEM(wide, BF)], 2,
    )
    if permuted:
        chunks = dict(d=Scatter(line, "d", *d_down))
        out_got = swap(out_send, "out")
    grad_x2, small, ffg, *d_up = line.call(
        functools.partial(ffn_back_kernel, base(SCATTER_KIND["u"])), "ffn_back",
        [order, info, up, grad_hidden, g_full, x2, normed3, vecs],
        [(wide, F32), vec, units, *blocks(16, FF)],
        [pltpu.VMEM((D, FF), BF)], 2,
    )

    def cross_back():
        return line.call(
            functools.partial(cross_back_kernel, base(SCATTER_KIND["c"])), "cross_back",
            [
                order, info, weights2, weights1, x1, normed2, mem, cq, ck, cv, mixed1, mixed2, log2, mask, grad_x2,
                vecs, small,
            ],
            [(wide, F32), (wide, BF), ((sources, D), F32), ((sources, D), BF), vec, *blocks(16, 2560)],
            [
                pltpu.VMEM((D, 2560), BF), pltpu.VMEM(wide, BF), pltpu.VMEM(wide, BF),
                pltpu.VMEM((src, D), BF), pltpu.VMEM((src, D), BF), pltpu.VMEM((src, D), F32),
            ],
            2,
        )

    def self_back(grad_x1, grad_mixed1, small):
        return line.call(
            functools.partial(self_back_kernel, base(SCATTER_KIND["s"])), "self_back",
            [order, info, weights1, x0, normed1, q, k, v, log1, grad_x1, grad_mixed1, vecs, small, ffg],
            [((rows, D), F32), ((rows, D), BF), *blocks(16, 1664)],
            [
                pltpu.VMEM((D, 1536), BF), pltpu.VMEM((BLOCKS, 16, 128), BF), pltpu.VMEM((16, D), F32),
                pltpu.VMEM(wide, BF), pltpu.VMEM(wide, BF), pltpu.VMEM(wide, BF), pltpu.VMEM(wide, F32),
            ],
            2,
        )

    def both(kept, got, name):
        return line.call(halves_kernel, f"halves_{name}", [info, kept, got], [((2,) + kept.shape, kept.dtype)], (), 1)[0]

    if permuted:
        chunks["u"] = Scatter(line, "u", *d_up)
        lasts = dict(
            d=(last_kernel, [((4, 16, D), F32)]),
            u=(last_kernel, [((16, FF), F32)]),
            c=(last_cross_kernel, [((16, n), F32) for n in (512, 1024, 512, 512)]),
            s=(last_self_kernel, [((16, 1536), F32), ((3, 16), F32), ((16, 10), F32), ((1, 64), F32)]),
        )
        done = {}
        for name, cost in plan(SCATTER):
            if name == "X":
                grad_x1, grad_mixed1, mem_keep, mem_send, small, *d_cross = cross_back()
                chunks["c"] = Scatter(line, "c", *d_cross)
                mem_got = swap(mem_send, "memory")
            elif name == "Y":
                in_keep, in_send, *d_self = self_back(grad_x1, grad_mixed1, small)
                chunks["s"] = Scatter(line, "s", *d_self)
                in_got = swap(in_send, "hidden")
            elif name == "o":
                output = both(out_keep, out_got, "out")
            elif name == "m":
                grad_memory = both(mem_keep, mem_got, "memory")
            elif name == "h":
                grad_hidden_in = both(in_keep, in_got, "hidden")
            elif chunks[name].hop:
                chunks[name].step(cost)
            else:
                kernel, shapes = lasts[name]
                mine = [me] if name == "s" else []
                done[name] = line.call(
                    kernel, f"last_{name}", [*mine, chunks[name].own, chunks[name].coming], shapes,
                    scalars=len(mine), flops=cost,
                )
        g_cq, g_ckv, g_co, g_out = done["c"]
        g_qkv, g_gains, g_biases, g_units = done["s"]
        rest = (
            g_qkv, g_out, g_cq, g_ckv, g_co, done["u"][0], done["d"][0].reshape(64, D), g_gains.T, g_biases,
            g_units.reshape(64),
        )
    else:
        grad_x1, grad_mixed1, mem_keep, mem_send, small, *d_cross = cross_back()
        in_keep, in_send, *d_self = self_back(grad_x1, grad_mixed1, small)
        output = both(out_keep, swap(out_send, "out"), "out")
        grad_memory = both(mem_keep, swap(mem_send, "memory"), "memory")
        grad_hidden_in = both(in_keep, swap(in_send, "hidden"), "hidden")
        d_down, d_up, d_cross, d_self = (d[0].astype(F32) for d in (d_down, d_up, d_cross, d_self))
        d_small = d_self[:, :, 1536:]
        columns = jnp.concatenate([d_small[i, :13, 16 * (i % 8) : 16 * (i % 8) + 16].T for i in range(BLOCKS)])
        d_unit = jnp.concatenate([d_small[i, 13, 64 * (i % 2) : 64 * (i % 2) + 64] for i in range(BLOCKS)])
        d_cross = d_cross.reshape(D, 2560)
        rest = tuple(
            lax.psum_scatter(d, BOTH, scatter_dimension=0, tiled=True)
            for d in (
                d_self[:, :, :1536].reshape(D, 1536), d_cross[:, 2048:], d_cross[:, :512], d_cross[:, 512:1536],
                d_cross[:, 1536:2048], d_up.reshape(D, FF), d_down.reshape(FF, D), columns[:, 10:], columns[:, :10],
                d_unit,
            )
        )
    return (output, grad_hidden_in, grad_memory) + rest


def solution(mesh):
    rows = P(BOTH, None)
    part = P("batch", "seq", None)
    return jax.shard_map(
        functools.partial(per_device, mesh.devices.size),
        mesh=mesh,
        in_specs=(part, part, P("batch"), P("batch", None), part) + (rows,) * 9 + (P(BOTH),),
        out_specs=(part, part, part) + (rows,) * 9 + (P(BOTH),),
        check_vma=False,
    )
```

```python
import functools

import jax
import jax.numpy as jnp
from jax import lax
from jax.experimental import pallas as pl
from jax.experimental.pallas import tpu as pltpu
from jax.sharding import PartitionSpec as P

D = 512
FF = 2048
HEADS = 8
HEAD_DIM = 64
EPSILON = 1e-05
NEGATIVE = -1000000000.0
SCALE = HEAD_DIM ** (-0.5)
BLOCKS = 32
WIDE = 4096
BF = jnp.bfloat16
F32 = jnp.float32
BOTH = ("batch", "seq")

QKV, OUT, CQ, CKV, CO = (0, 1536), (1536, 2048), (2048, 2560), (2560, 3584), (3584, 4096)


def dot(a, b):
    return lax.dot_general(a, b, (((1,), (0,)), ((), ())), preferred_element_type=F32)


def dot_nt(a, b):
    return lax.dot_general(a, b, (((1,), (1,)), ((), ())), preferred_element_type=F32)


def dot_tn(a, b):
    return lax.dot_general(a, b, (((0,), (0,)), ((), ())), preferred_element_type=F32)


def norm(values):
    centred = values - jnp.mean(values, axis=-1, keepdims=True)
    rate = lax.rsqrt(jnp.mean(centred * centred, axis=-1, keepdims=True) + EPSILON)
    return centred * rate, rate


def norm_back(values, gain, grad):
    unit, rate = norm(values)
    scaled = grad * gain
    part = rate * (
        scaled
        - jnp.mean(scaled, axis=-1, keepdims=True)
        - unit * jnp.mean(scaled * unit, axis=-1, keepdims=True)
    )
    return part, row_sum(grad * unit), row_sum(grad)


def row_sum(values):
    return jnp.sum(values.astype(F32), axis=0, keepdims=True)


def lane_masks(dtype):
    lane = lax.broadcasted_iota(jnp.int32, (1, 128), 1)
    return [(lane // HEAD_DIM == j).astype(dtype) for j in range(2)]


def scores_t(keys, queries, visible):
    return jnp.where(visible, dot_nt(keys, queries) * SCALE, NEGATIVE)


def attend(q_ref, k_ref, v_ref, visible, mixed_ref, probs_ref):
    masks = lane_masks(BF)
    for pair in range(HEADS // 2):
        cols = slice(128 * pair, 128 * pair + 128)
        queries, keys, values = q_ref[:, cols], k_ref[:, cols], v_ref[:, cols]
        total = None
        for j in range(2):
            scores = scores_t(keys, queries * masks[j], visible)
            top = jnp.max(scores, axis=0, keepdims=True)
            exponent = jnp.exp(scores - top)
            row_total = jnp.sum(exponent, axis=0, keepdims=True)
            probs = (exponent * (1.0 / row_total)).astype(BF)
            probs_ref[2 * pair + j] = probs
            part = dot_tn(probs, values * masks[j])
            total = part if total is None else total + part
        mixed_ref[:, cols] = total.astype(BF)


def attend_back(q_ref, k_ref, v_ref, probs_ref, mixed_ref, grad_ref, dq_ref, dk_ref, dv_ref):
    masks = lane_masks(BF)
    product = grad_ref[...].astype(F32) * mixed_ref[...].astype(F32)
    high = product.astype(BF)
    low = (product - high.astype(F32)).astype(BF)
    head = lax.broadcasted_iota(jnp.int32, (HEADS, D), 0)
    picks = (lax.broadcasted_iota(jnp.int32, (HEADS, D), 1) // HEAD_DIM == head).astype(BF)
    inner = dot_nt(picks, high) + dot_nt(picks, low)
    for pair in range(HEADS // 2):
        cols = slice(128 * pair, 128 * pair + 128)
        queries, keys, values, grads = q_ref[:, cols], k_ref[:, cols], v_ref[:, cols], grad_ref[:, cols]
        dq = dk = dv = None
        for j in range(2):
            own_q, own_k, own_g = queries * masks[j], keys * masks[j], grads * masks[j]
            probs = probs_ref[2 * pair + j]
            grad_probs = dot_nt(values, own_g)
            part_v = dot(probs, own_g)
            low = (probs.astype(F32) * (grad_probs - inner[2 * pair + j : 2 * pair + j + 1, :])).astype(BF)
            part_k = dot(low, own_q)
            part_q = dot_tn(low, own_k)
            dq = part_q if dq is None else dq + part_q
            dk = part_k if dk is None else dk + part_k
            dv = part_v if dv is None else dv + part_v
        dq_ref[:, cols] = (dq * SCALE).astype(BF)
        dk_ref[:, cols] = (dk * SCALE).astype(BF)
        dv_ref[:, cols] = dv.astype(BF)


def place_blocks(order, base, pieces, put):
    for i, piece in enumerate(pieces):
        if piece is None:
            continue
        count = piece.shape[0]

        @pl.loop(0, count)
        def _(b, piece=piece, first=base + i * count):
            put(piece, b, order[first + b])


def rows16(index):
    return pl.ds(pl.multiple_of(index * 16, 16), 16)


def halves(ref, place, rows):
    own = pl.ds(pl.multiple_of(place * rows, rows), rows)
    other = pl.ds(pl.multiple_of((1 - place) * rows, rows), rows)
    return ref.at[own], ref.at[other]


def self_visible(length, rows):
    key = lax.broadcasted_iota(jnp.int32, (rows, rows), 0)
    query = lax.broadcasted_iota(jnp.int32, (rows, rows), 1)
    return (key <= query) & (key < length)


def cross_visible(mask):
    row = jnp.broadcast_to(mask[...].astype(F32), (8, mask.shape[1]))
    column = row.T[:, 0:1]
    return (column > 0) | (lax.broadcasted_iota(jnp.int32, column.shape, 0) == 0)


def pack_kernel(
    me, all_lengths, all_units, gains, biases, qkv, out, cq, ckv, co, up, down, hidden, memory, grads, masks,
    order, info, attention, w_up, w_down, sent, kept, mask, token, rows, gain_rows, bias_rows, lengths, units, sems,
):
    index = me[0]
    core = (index // 2) % 2
    place = index % 2
    far = 1 - place
    moves = [(gains, gain_rows), (biases, bias_rows), (masks.at[pl.ds(place, 1)], mask), (up, w_up), (down, w_down)]
    moves += [(all_lengths, lengths), (all_units, units)]
    first = 0
    for part in (hidden, memory, grads):
        last = first + part.shape[1]
        moves.append((part.at[far], sent.at[first:last]))
        moves.append((part.at[place], kept.at[first:last]))
        first = last
    first = 0
    for part in (qkv, out, cq, ckv, co):
        width = part.shape[1]
        moves.append((part, attention.at[0, :, first : first + width]))
        first += width
    moves = [pltpu.make_async_copy(a, b, sems.at[i]) for i, (a, b) in enumerate(moves)]
    for move in moves:
        move.start()
    info[0] = place
    for kind, both in enumerate(FLIPS):
        for k in range(16):
            plane = [sum(((k >> b) & 1) * flip for b, flip in enumerate(flips)) for flips in both]
            order[BLOCKS * kind + k] = index ^ jnp.where(core == 0, plane[0], plane[1])
            order[BLOCKS * kind + 16 + k] = index ^ jnp.where(core == 0, plane[1] | 2, plane[0] | 2)
    token[...] = jnp.zeros_like(token)
    rows[...] = jnp.zeros_like(rows)
    lane = lax.broadcasted_iota(jnp.int32, (16, 128), 1)
    spread = (lane % 16 == lax.broadcasted_iota(jnp.int32, (16, 128), 0)).astype(BF)
    unit_lane = lax.broadcasted_iota(jnp.int32, (64, 128), 1)
    unit_spread = (unit_lane % 64 == lax.broadcasted_iota(jnp.int32, (64, 128), 0)).astype(BF)
    for move in moves:
        move.wait()
    info[1] = lengths[place]
    rows[13:14, :] = dot(jnp.broadcast_to(units[...], (16, 64)), unit_spread)[0:1, :]
    rows[0:10, :] = dot_tn(bias_rows[...], spread)
    rows[10:13, :] = dot(gain_rows[...], spread)
    attention[0, :, WIDE : WIDE + 128] = rows[...].astype(BF)


def join_kernel(have, got, extra, joined):
    count = have.shape[0]
    joined[0:count] = have[...]
    joined[count:] = got[...]


def pass_kernel(value, out):
    out[...] = value[...]


def add_kernel(axis, *refs):
    *parts, send, keep = refs
    count = send.shape[0]
    first = 0
    for own, got in zip(parts[::2], parts[1::2]):
        last = first + own.shape[axis]
        place = (slice(None),) * axis + (slice(first, last),)
        send[place] = (own[count:].astype(F32) + got[count:].astype(F32)).astype(send.dtype)
        keep[place] = (own[:count].astype(F32) + got[:count].astype(F32)).astype(keep.dtype)
        first = last


def last_ffn_kernel(*refs):
    (*parts, d_up, d_down) = refs
    total = [own[0] + got[0].astype(F32) for own, got in zip(parts[::2], parts[1::2])]
    total = total[0] if len(total) == 1 else jnp.concatenate(total, axis=0)
    for group in range(4):
        d_up[:, 512 * group : 512 * group + 512] = total[group]
        d_down[16 * group : 16 * group + 16, :] = total[4 + group]


def last_attention_kernel(me, *refs):
    (*parts, d_cq, d_ckv, d_co, d_out, d_qkv, d_gains, d_biases, d_units) = refs
    total = [own[0] + got[0].astype(F32) for own, got in zip(parts[::2], parts[1::2])]
    total = total[0] if len(total) == 1 else jnp.concatenate(total, axis=1)
    d_cq[...] = total[:, 0:512]
    d_ckv[...] = total[:, 512:1536]
    d_co[...] = total[:, 1536:2048]
    d_out[...] = total[:, 2048:2560]
    d_qkv[...] = total[:, 2560:4096]
    small = total[:, 4096:4224]
    index = me[0]
    vectors = pltpu.roll(small, (128 - 16 * (index % 8)) % 128, 1)[:, 0:16]
    d_gains[...] = vectors[10:13, :]
    d_biases[...] = vectors.T[:, 0:10]
    d_units[...] = pltpu.roll(small, (128 - 64 * (index % 2)) % 128, 1)[13:14, 0:64]


def halves_kernel(info, kept, got, out):
    place = info[0]
    out[place] = kept[...]
    out[1 - place] = got[...].astype(out.dtype)


def self_forward_kernel(
    base, order, info, p0, p1, p2, p3, kept, new, weights, vecs, ffb, x0, normed1, q, k, v, mixed1, probs1, x1, normed2,
    small,
):
    place, length = info[0], info[1]

    def put(piece, b, index):
        weights[rows16(index), :] = piece[b, :, 0:2048]
        small[index] = piece[b, :, WIDE : WIDE + 128]

    place_blocks(order, base, (p0, p1, p2, p3), put)
    rows = x0.shape[0] // 2
    own, other = halves(x0, place, rows)
    own[...], other[...] = kept[0:rows], new[0:rows]
    hidden = x0[...].astype(F32)
    lane = lax.broadcasted_iota(jnp.int32, (16, 128), 1)
    for tile in range(D // 128):
        row = jnp.zeros((16, 128), F32)
        for i in range(8):
            row = jnp.where(lane // 16 == i, small[8 * tile + i].astype(F32), row)
        vecs[:, 128 * tile : 128 * tile + 128] = row
    ffb[...] = jnp.zeros_like(ffb)
    for tile in range(FF // 128):
        row = jnp.where(lane < 64, small[2 * tile].astype(F32), small[2 * tile + 1].astype(F32))
        ffb[tile // 4 : tile // 4 + 1, 128 * (tile % 4) : 128 * (tile % 4) + 128] = row[13:14, :]

    def bias(j):
        return vecs[j : j + 1, :]

    normed1[...] = (norm(hidden)[0] * bias(10) + bias(0)).astype(BF)
    q[...] = (dot(normed1[...], weights[:, 0:512]) + bias(1)).astype(BF)
    k[...] = dot(normed1[...], weights[:, 512:1024]).astype(BF)
    v[...] = (dot(normed1[...], weights[:, 1024:1536]) + bias(2)).astype(BF)
    attend(q, k, v, self_visible(length, 2 * rows), mixed1, probs1)
    after_self = hidden + (dot(mixed1[...], weights[:, 1536:2048]) + bias(3))
    x1[...] = after_self
    normed2[...] = (norm(after_self)[0] * bias(11) + bias(4)).astype(BF)


def cross_forward_kernel(
    base, order, info, p0, p1, p2, p3, kept, new, mask, vecs, x1, normed2,
    weights, mem, cq, ck, cv, mixed2, probs2, x2, normed3,
):
    place = info[0]

    def put(piece, b, index):
        weights[rows16(index), :] = piece[b, :, 2048:4096]

    place_blocks(order, base, (p0, p1, p2, p3), put)
    sources = mem.shape[0] // 2
    first = x1.shape[0] // 2
    own, other = halves(mem, place, sources)
    own[...], other[...] = kept[first : first + sources], new[first : first + sources]

    def bias(j):
        return vecs[j : j + 1, :]

    ck[...] = dot(mem[...], weights[:, 512:1024]).astype(BF)
    cv[...] = (dot(mem[...], weights[:, 1024:1536]) + bias(6)).astype(BF)
    cq[...] = (dot(normed2[...], weights[:, 0:512]) + bias(5)).astype(BF)
    attend(cq, ck, cv, cross_visible(mask), mixed2, probs2)
    after_cross = x1[...] + (dot(mixed2[...], weights[:, 1536:2048]) + bias(7))
    x2[...] = after_cross
    normed3[...] = (norm(after_cross)[0] * bias(12) + bias(8)).astype(BF)


def four_rows(index):
    return pl.ds(pl.multiple_of(index * 4, 4), 4)


def ffn_kernel(
    bases, order, info, u0, u1, u2, u3, w0, w1, w2, w3, x2, normed3, kept, new, vecs, ffb,
    out_keep, out_send, up, grad_hidden, grad_out, own_out, other_out,
    down, d_down, result,
):
    place = info[0]

    def put_up(piece, b, index):
        up[rows16(index), :] = piece[b]

    def put_down(piece, b, index):
        down[four_rows(index)] = piece[b]

    place_blocks(order, bases[0], (u0, u1, u2, u3), put_up)
    place_blocks(order, bases[1], (w0, w1, w2, w3), put_down)
    rows = out_keep.shape[0]
    first = kept.shape[0] - rows
    own, other = halves(grad_out, place, rows)
    own[...], other[...] = kept[first:], new[first:]
    grads = grad_out[...]
    normed = normed3[...]
    total = None
    c0 = (2.0 / jnp.pi) ** 0.5
    for group in range(FF // 512):
        w_down = down[32 * group : 32 * group + 32].reshape(512, D)
        hidden = dot(normed, up[:, 512 * group : 512 * group + 512]) + ffb[group : group + 1, :]
        square = hidden * hidden
        tanh = jnp.tanh(c0 * (hidden + 0.044715 * (square * hidden)))
        half = 0.5 * (1.0 + tanh)
        active = (hidden * half).astype(BF)
        slope = half + hidden * (0.5 * c0) * (1.0 - tanh * tanh) * (1.0 + (3 * 0.044715) * square)
        part = dot(active, w_down)
        total = part if total is None else total + part
        grad_hidden[:, 512 * group : 512 * group + 512] = (slope * dot_nt(grads, w_down)).astype(BF)
        d_down[32 * group : 32 * group + 32] = dot_tn(active, grads).astype(BF).reshape(32, 16, D)
    take_blocks(order, bases[2], (own_out, other_out), lambda index: d_down[four_rows(index)])
    result[...] = (x2[...] + (total + vecs[9:10, :])).astype(BF)
    own, other = halves(result, place, rows)
    out_keep[...], out_send[...] = own[...], other[...]


def ffn_back_kernel(
    base, order, info, up, grad_hidden, grad_out, x2, normed3, vecs, grad_x2, small, ffg, own_out, other_out, d_up
):
    normed_t = normed3[...].T
    grad_normed = None
    ffg[...] = jnp.zeros_like(ffg)
    for group in range(FF // 512):
        grad = grad_hidden[:, 512 * group : 512 * group + 512]
        d_up[group] = dot(normed_t, grad).astype(BF)
        ffg[group : group + 1, :] = row_sum(grad)
        part = dot_nt(grad, up[:, 512 * group : 512 * group + 512])
        grad_normed = part if grad_normed is None else grad_normed + part
    take_blocks(order, base, (own_out, other_out), lambda index: d_up[:, rows16(index), :])
    part, d_gain, d_shift = norm_back(x2[...], vecs[12:13, :], grad_normed)
    grads = grad_out[...]
    grad_x2[...] = grads.astype(F32) + part
    small[...] = jnp.zeros_like(small)
    small[12:13, :] = d_gain
    small[8:9, :] = d_shift
    small[9:10, :] = row_sum(grads)


def cross_back_kernel(
    base, order, info, weights, weights1, x1, normed2, mem, cq, ck, cv, mixed1, mixed2, probs2, grad_x2, vecs, small_in,
    grad_x1, grad_mixed1, mem_keep, mem_send, small, own_out, other_out,
    d_weights, grad_mixed, dq, dk, dv, grad_mem,
):
    place = info[0]
    small[...] = small_in[...]
    grad_y = grad_x2[...].astype(BF)
    d_weights[:, 1536:2048] = dot_tn(mixed2[...], grad_y).astype(BF)
    small[7:8, :] = row_sum(grad_y)
    grad_mixed[...] = dot_nt(grad_y, weights[:, 1536:2048]).astype(BF)
    attend_back(cq, ck, cv, probs2, mixed2, grad_mixed, dq, dk, dv)
    memory_t = mem[...].T
    d_weights[:, 512:1024] = dot(memory_t, dk[...]).astype(BF)
    d_weights[:, 1024:1536] = dot(memory_t, dv[...]).astype(BF)
    d_weights[:, 0:512] = dot_tn(normed2[...], dq[...]).astype(BF)
    small[6:7, :] = row_sum(dv[...])
    small[5:6, :] = row_sum(dq[...])
    grad_mem[...] = dot_nt(dk[...], weights[:, 512:1024]) + dot_nt(dv[...], weights[:, 1024:1536])
    own, other = halves(grad_mem, place, mem_keep.shape[0])
    mem_keep[...] = own[...]
    mem_send[...] = other[...].astype(BF)
    part, d_gain, d_shift = norm_back(x1[...], vecs[11:12, :], dot_nt(dq[...], weights[:, 0:512]))
    small[11:12, :] = d_gain
    small[4:5, :] = d_shift
    total = grad_x2[...] + part
    grad_x1[...] = total
    grad_y = total.astype(BF)
    d_weights[:, 2048:2560] = dot_tn(mixed1[...], grad_y).astype(BF)
    small[3:4, :] = row_sum(grad_y)
    grad_mixed1[...] = dot_nt(grad_y, weights1[:, 1536:2048]).astype(BF)
    take_blocks(order, base, (own_out, other_out), lambda index: d_weights[rows16(index), :])


def self_back_kernel(
    base, order, info, weights, x0, normed1, q, k, v, mixed1, probs1, grad_x1, grad_mixed, vecs, small_in, ffg,
    in_keep, in_send, own_out, other_out,
    d_weights, d_small, small, dq, dk, dv, grad_in,
):
    place = info[0]
    small[...] = small_in[...]
    rows = q.shape[0]
    attend_back(q, k, v, probs1, mixed1, grad_mixed, dq, dk, dv)
    normed_t = normed1[...].T
    for i, part in enumerate((dq, dk, dv)):
        d_weights[:, 512 * i : 512 * i + 512] = dot(normed_t, part[...]).astype(BF)
    small[1:2, :] = row_sum(dq[...])
    small[2:3, :] = row_sum(dv[...])
    grad_normed = (
        dot_nt(dq[...], weights[:, 0:512])
        + dot_nt(dk[...], weights[:, 512:1024])
        + dot_nt(dv[...], weights[:, 1024:1536])
    )
    part, d_gain, d_shift = norm_back(x0[...].astype(F32), vecs[10:11, :], grad_normed)
    small[10:11, :] = d_gain
    small[0:1, :] = d_shift
    for index in range(BLOCKS):
        tile = 128 * (index // 8)
        d_small[index] = small[:, tile : tile + 128].astype(BF)
        group, tile = index // 8, 128 * ((index // 2) % 4)
        d_small[index, 13:14, :] = ffg[group : group + 1, tile : tile + 128].astype(BF)
    first = base
    for out in (own_out, other_out):
        if out is None:
            continue

        @pl.loop(0, out.shape[0])
        def _(b, out=out, first=first):
            index = order[first + b]
            out[b, :, 0:1536] = d_weights[rows16(index), :]
            out[b, :, 1536:1664] = d_small[index]

        first += out.shape[0]
    grad_in[...] = grad_x1[...] + part
    own, other = halves(grad_in, place, rows // 2)
    in_keep[...] = own[...]
    in_send[...] = other[...].astype(BF)


def take_blocks(order, base, outs, take):
    first = base
    for out in outs:
        if out is None:
            continue

        @pl.loop(0, out.shape[0])
        def _(b, out=out, first=first):
            out[b] = take(order[first + b])

        first += out.shape[0]


VMEM = pl.BlockSpec(memory_space=pltpu.VMEM)
SMEM = pl.BlockSpec(memory_space=pltpu.SMEM)
HBM = pl.BlockSpec(memory_space=pltpu.HBM)


def shape(dims, dtype):
    return jax.ShapeDtypeStruct(dims, dtype)


EVENT = 1_000_000_000


class Line:
    def __init__(self):
        self.token = None

    def call(self, kernel, name, inputs, outs, scratch=(), scalars=0, flops=1):
        given = [i for i in inputs if i is not None]
        made = [o for o in outs if o is not None]
        tokens = [self.token] if self.token is not None else []

        def body(*refs):
            refs = list(refs)
            taken = [None if i is None else refs.pop(0) for i in inputs]
            for _ in tokens:
                refs.pop(0)
            given_out = [None if o is None else refs.pop(0) for o in outs]
            out_token = refs.pop(0)
            out_token[...] = jnp.zeros_like(out_token)
            kernel(*taken, *given_out, *refs)

        moved = sum(a.size * a.dtype.itemsize for a in given)
        *results, self.token = pl.pallas_call(
            body,
            name=name,
            out_shape=[shape(*o) for o in made] + [shape((8, 128), F32)],
            in_specs=[SMEM] * scalars + [VMEM] * (len(given) - scalars + len(tokens)),
            out_specs=[VMEM] * (len(made) + 1),
            scratch_shapes=list(scratch),
            compiler_params=pltpu.CompilerParams(vmem_limit_bytes=32 * 1024 * 1024),
            cost_estimate=pl.CostEstimate(flops=flops, bytes_accessed=1, transcendentals=0),
        )(*given, *tokens)
        results = iter(results)
        return [None if o is None else next(results) for o in outs]


def flat_index(z, y, c, x):
    return ((z * 2 + y) * 2 + c) * 2 + x


def pairs_of(move):
    pairs = []
    for z in range(4):
        for y in range(2):
            for c in range(2):
                for x in range(2):
                    pairs.append((flat_index(z, y, c, x), flat_index(*move(z, y, c, x))))
    return pairs


CORE = pairs_of(lambda z, y, c, x: (z, y, 1 - c, x))
SIDE = pairs_of(lambda z, y, c, x: (z, y, c, 1 - x))
HOP_Z1 = pairs_of(lambda z, y, c, x: (z ^ 1 if c == 0 else z ^ 2, y, c, x))
HOP_Z2 = pairs_of(lambda z, y, c, x: (z ^ 2 if c == 0 else z ^ 1, y, c, x))
HOP_P1 = pairs_of(lambda z, y, c, x: (z, y, c, 1 - x) if c == 0 else (z, 1 - y, c, x))
HOP_P2 = pairs_of(lambda z, y, c, x: (z, y, c, 1 - x) if c == 1 else (z, 1 - y, c, x))
HOPS = (
    (HOP_Z1, HOP_Z2, HOP_P1, HOP_P2),
    (HOP_P1, HOP_P2, HOP_Z1, HOP_Z2),
    (HOP_P1, HOP_Z1, HOP_Z2, HOP_P2),
)
FLIPS = (
    ((8, 16, 1, 4), (16, 8, 4, 1)),
    ((1, 4, 8, 16), (4, 1, 16, 8)),
    ((1, 8, 16, 4), (4, 16, 8, 1)),
)
GATHER_KIND = dict(a=0, u=0, w=1)
GATHER = (
    ("a", 12), ("w", 12), ("u", 12), ("a", 12), ("w", 12), ("u", 12), ("a", 12), ("w", 12), ("u", 12),
)
SCATTER_KIND = dict(d=2, u=2, f=2, c=0, s=0, a=0)
SCATTER = (
    ("d", 0), ("u", 0), ("X", 0), ("Y", 0), ("d", 12), ("u", 0), ("c", 3),
    ("s", 0), ("d", 0.3), ("o", 4), ("s", 0.6), ("c", 0), ("u", 0), ("s", 0.3),
    ("d", 1.5), ("c", 0), ("u", 0), ("s", 1.5), ("c", 0), ("m", 0), ("udf", 0),
    ("f", 0.6), ("h", 0), ("csa", 0), ("a", 0),
)


def permute(value, pairs):
    return lax.ppermute(value, BOTH, pairs)


class Gather:
    def __init__(self, line, name, own):
        self.line, self.name, self.have, self.hop = line, name, own, 0
        self.hops = HOPS[GATHER_KIND[name]]

    def start(self):
        with jax.named_scope(f"gather_{self.name}_hop{self.hop}"):
            self.coming = permute(self.have, self.hops[self.hop])
        self.hop += 1
        if self.hop == 4:
            with jax.named_scope(f"gather_{self.name}_core0"):
                self.core = permute(self.have, CORE)

    def step(self, extra, cost):
        dims = self.have.shape
        (self.have,) = self.line.call(
            join_kernel, f"join_{self.name}{self.hop}", [self.have, self.coming, extra],
            [((2 * dims[0],) + dims[1:], BF)], flops=cost,
        )
        self.start()

    def finish(self, tied=False):
        if tied:
            (self.coming,) = self.line.call(
                pass_kernel, f"pass_{self.name}", [self.coming], [(self.coming.shape, BF)], flops=12 * EVENT
            )
        with jax.named_scope(f"gather_{self.name}_core1"):
            return [self.have, self.coming, self.core, permute(self.coming, CORE)]


class Scatter:
    def __init__(self, line, name, hop, parts):
        self.line, self.name, self.hop, self.parts = line, name, hop, parts
        self.hops, self.axis = HOPS[SCATTER_KIND[name]], (1 if name in "duf" else 2)

    @classmethod
    def begin(cls, line, name, own, other):
        with jax.named_scope(f"scatter_{name}_core"):
            return cls(line, name, 4, [(own, permute(other, CORE))])

    def step(self, cost):
        self.hop -= 1
        dims = list(self.parts[0][0].shape)
        dims[0], dims[self.axis] = 1 << self.hop, sum(own.shape[self.axis] for own, _ in self.parts)
        send, own = self.line.call(
            functools.partial(add_kernel, self.axis), f"add_{self.name}{self.hop}", [v for p in self.parts for v in p],
            [(tuple(dims), BF), (tuple(dims), BF if self.hop else F32)], flops=cost,
        )
        with jax.named_scope(f"scatter_{self.name}_hop{self.hop}"):
            self.parts = [(own, permute(send, self.hops[self.hop]))]


def small_rows(biases, gains, ffn_bias):
    count = biases.shape[0]
    columns = jnp.concatenate([biases, gains], axis=2).transpose(0, 2, 1)
    rows = jnp.tile(columns, (1, 1, 8))
    units = jnp.tile(ffn_bias.reshape(count, 1, 64), (1, 1, 2))
    return jnp.concatenate([rows, units, jnp.zeros((count, 2, 128), BF)], axis=1)


def pack_attention(qkv, out, cq, ckv, co, small):
    return jnp.concatenate([qkv, out, cq, ckv, co, small], axis=2)


def packed(hidden_in, memory, lengths, source_mask, grad_out, params, me):
    (w_qkv, w_out, w_cq, w_ckv, w_co, w_up, w_down, gains, biases, ffn_bias) = params
    rows = 2 * hidden_in.shape[1] + memory.shape[1]
    return pl.pallas_call(
        pack_kernel,
        name="pack",
        out_shape=[
            shape((len(FLIPS) * BLOCKS,), jnp.int32), shape((2,), jnp.int32), shape((1, 16, WIDE + 128), BF),
            shape((16, FF), BF), shape((64, D), BF), shape((rows, D), BF), shape((rows, D), BF),
            shape((1, source_mask.shape[1]), jnp.int32), shape((8, 128), F32),
        ],
        in_specs=[SMEM] + [HBM] * 15,
        out_specs=[SMEM, SMEM] + [VMEM] * 7,
        scratch_shapes=[
            pltpu.VMEM((16, 128), F32), pltpu.VMEM((3, 16), BF), pltpu.VMEM((16, 10), BF),
            pltpu.SMEM(lengths.shape, jnp.int32), pltpu.VMEM((1, 64), BF), pltpu.SemaphoreType.DMA((18,)),
        ],
        compiler_params=pltpu.CompilerParams(vmem_limit_bytes=16 * 1024 * 1024),
    )(
        me,
        *(
            pltpu.with_memory_space_constraint(v, pltpu.HBM)
            for v in (
                lengths, ffn_bias.reshape(1, 64), gains.T, biases, w_qkv, w_out, w_cq, w_ckv, w_co, w_up, w_down, hidden_in, memory, grad_out, source_mask,
            )
        ),
    )


def per_device(n_devices, hidden_in, memory, lengths, source_mask, grad_out, *params):
    permuted = n_devices == BLOCKS
    rows, sources = hidden_in.shape[1], memory.shape[1]
    tgt, src = 2 * rows, 2 * sources
    line = Line()

    def swap(value, name):
        with jax.named_scope(f"swap_{name}"):
            return lax.ppermute(value, "seq", [(0, 1), (1, 0)])

    place = lax.axis_index("seq")
    if permuted:
        me = lax.axis_index(BOTH).astype(jnp.int32).reshape(1)
        order, info, attention, w_up, w_down, sent, kept, mask, line.token = packed(
            hidden_in, memory, lengths, source_mask, grad_out, params, me
        )
        chunks = dict(
            a=Gather(line, "a", attention), w=Gather(line, "w", w_down.reshape(1, 4, 16, D)),
            u=Gather(line, "u", w_up[None]),
        )
        chunks["a"].start()
        chunks["w"].start()
        new = swap(sent, "in")
        chunks["u"].start()
        for name, cost in GATHER:
            chunks[name].step(new if name == "a" and chunks[name].hop == 2 else None, int(cost * EVENT))
        a_pieces = chunks["a"].finish()
        halves_of = (16, 16)
        base = lambda kind: BLOCKS * kind
    else:
        params = [lax.all_gather(p, BOTH, axis=0, tiled=True) for p in params]
        (w_qkv, w_out, w_cq, w_ckv, w_co, w_up, w_down, gains, biases, ffn_bias) = params
        cut = lambda w: w.reshape(BLOCKS, -1, w.shape[1])
        attention = pack_attention(
            *(cut(w) for w in (w_qkv, w_out, w_cq, w_ckv, w_co)), small_rows(cut(biases), cut(gains), ffn_bias)
        )
        pick = lambda v, i: lax.dynamic_index_in_dim(v, i, 0, keepdims=False)
        both_of = lambda i: jnp.concatenate([pick(v, i) for v in (hidden_in, memory, grad_out)], axis=0)
        kept, new = both_of(place), swap(both_of(1 - place), "in")
        mask = pick(source_mask, place)[None]
        info = jnp.stack([place, pick(lengths, place)]).astype(jnp.int32)
        order = jnp.arange(BLOCKS, dtype=jnp.int32)
        a_pieces = [attention, None, None, None]
        halves_of = (BLOCKS, None)
        base = lambda kind: 0

    wide = (tgt, D)
    vec = ((16, D), F32)
    units = ((8, 512), F32)
    blocks = lambda *dims: [None if n is None else ((n,) + dims, BF) for n in halves_of]
    weights1, vecs, ffb, x0, normed1, q, k, v, mixed1, probs1, x1, normed2 = line.call(
        functools.partial(self_forward_kernel, base(GATHER_KIND["a"])), "self_forward", [order, info, *a_pieces, kept, new],
        [
            ((D, 2048), BF), vec, units, (wide, BF), (wide, BF), (wide, BF), (wide, BF), (wide, BF), (wide, BF),
            ((HEADS, tgt, tgt), BF), (wide, F32), (wide, BF),
        ],
        [pltpu.VMEM((BLOCKS, 16, 128), BF)], 2,
    )
    if permuted:
        w_pieces = chunks["w"].finish(True)
    weights2, mem, cq, ck, cv, mixed2, probs2, x2, normed3 = line.call(
        functools.partial(cross_forward_kernel, base(GATHER_KIND["a"])), "cross_forward",
        [order, info, *a_pieces, kept, new, mask, vecs, x1, normed2],
        [
            ((D, 2048), BF), ((src, D), BF), (wide, BF), ((src, D), BF), ((src, D), BF), (wide, BF),
            ((HEADS, src, tgt), BF), (wide, F32), (wide, BF),
        ],
        [], 2,
    )
    if permuted:
        u_pieces = chunks["u"].finish(True)
    else:
        u_pieces, w_pieces = [cut(w_up), None, None, None], [w_down.reshape(BLOCKS, 4, 16, D), None, None, None]
    bases = (base(GATHER_KIND["u"]), base(GATHER_KIND["w"]), base(SCATTER_KIND["d"]))
    out_keep, out_send, up, grad_hidden, g_full, *d_down = line.call(
        functools.partial(ffn_kernel, bases), "ffn",
        [order, info, *u_pieces, *w_pieces, x2, normed3, kept, new, vecs, ffb],
        [((rows, D), BF), ((rows, D), BF), ((D, FF), BF), ((tgt, FF), BF), (wide, BF), *blocks(4, 16, D)],
        [pltpu.VMEM((128, 16, D), BF), pltpu.VMEM((128, 16, D), BF), pltpu.VMEM(wide, BF)], 2,
    )
    if permuted:
        chunks = dict(d=Scatter.begin(line, "d", *d_down))
        out_got = swap(out_send, "out")
    grad_x2, small, ffg, *d_up = line.call(
        functools.partial(ffn_back_kernel, base(SCATTER_KIND["u"])), "ffn_back",
        [order, info, up, grad_hidden, g_full, x2, normed3, vecs],
        [(wide, F32), vec, units, *blocks(4, 16, 512)],
        [pltpu.VMEM((4, D, 512), BF)], 2,
    )

    def cross_back():
        return line.call(
            functools.partial(cross_back_kernel, base(SCATTER_KIND["c"])), "cross_back",
            [
                order, info, weights2, weights1, x1, normed2, mem, cq, ck, cv, mixed1, mixed2, probs2, grad_x2, vecs,
                small,
            ],
            [(wide, F32), (wide, BF), ((sources, D), F32), ((sources, D), BF), vec, *blocks(16, 2560)],
            [
                pltpu.VMEM((D, 2560), BF), pltpu.VMEM(wide, BF), pltpu.VMEM(wide, BF),
                pltpu.VMEM((src, D), BF), pltpu.VMEM((src, D), BF), pltpu.VMEM((src, D), F32),
            ],
            2,
        )

    def self_back(grad_x1, grad_mixed1, small):
        return line.call(
            functools.partial(self_back_kernel, base(SCATTER_KIND["s"])), "self_back",
            [order, info, weights1, x0, normed1, q, k, v, mixed1, probs1, grad_x1, grad_mixed1, vecs, small, ffg],
            [((rows, D), F32), ((rows, D), BF), *blocks(16, 1664)],
            [
                pltpu.VMEM((D, 1536), BF), pltpu.VMEM((BLOCKS, 16, 128), BF), pltpu.VMEM((16, D), F32),
                pltpu.VMEM(wide, BF), pltpu.VMEM(wide, BF), pltpu.VMEM(wide, BF), pltpu.VMEM(wide, F32),
            ],
            2,
        )

    def both(kept, got, name):
        return line.call(halves_kernel, f"halves_{name}", [info, kept, got], [((2,) + kept.shape, kept.dtype)], (), 1)[0]

    if permuted:
        chunks["u"] = Scatter.begin(line, "u", *d_up)
        lasts = dict(
            f=(last_ffn_kernel, [((16, FF), F32), ((64, D), F32)]),
            a=(
                last_attention_kernel,
                [((16, n), F32) for n in (512, 1024, 512, 512, 1536)]
                + [((3, 16), F32), ((16, 10), F32), ((1, 64), F32)],
            ),
        )
        done = {}
        for name, cost in SCATTER:
            if name == "X":
                grad_x1, grad_mixed1, mem_keep, mem_send, small, *d_cross = cross_back()
                chunks["c"] = Scatter.begin(line, "c", *d_cross)
                mem_got = swap(mem_send, "memory")
            elif name == "Y":
                in_keep, in_send, *d_self = self_back(grad_x1, grad_mixed1, small)
                chunks["s"] = Scatter.begin(line, "s", *d_self)
                in_got = swap(in_send, "hidden")
            elif name == "o":
                output = both(out_keep, out_got, "out")
            elif name == "m":
                grad_memory = both(mem_keep, mem_got, "memory")
            elif name == "h":
                grad_hidden_in = both(in_keep, in_got, "hidden")
            elif len(name) > 1:
                first, second, joined = name
                hop = chunks[first].hop
                chunks[joined] = Scatter(line, joined, hop, chunks[first].parts + chunks[second].parts)
            elif chunks[name].hop:
                chunks[name].step(int(cost * EVENT))
            else:
                kernel, shapes = lasts[name]
                mine = [me] if name == "a" else []
                done[name] = line.call(
                    kernel, f"last_{name}", mine + [v for p in chunks[name].parts for v in p], shapes,
                    scalars=len(mine), flops=int(cost * EVENT),
                )
        g_up, g_down = done["f"]
        g_cq, g_ckv, g_co, g_out, g_qkv, g_gains, g_biases, g_units = done["a"]
        rest = (g_qkv, g_out, g_cq, g_ckv, g_co, g_up, g_down, g_gains.T, g_biases, g_units.reshape(64))
    else:
        grad_x1, grad_mixed1, mem_keep, mem_send, small, *d_cross = cross_back()
        in_keep, in_send, *d_self = self_back(grad_x1, grad_mixed1, small)
        output = both(out_keep, swap(out_send, "out"), "out")
        grad_memory = both(mem_keep, swap(mem_send, "memory"), "memory")
        grad_hidden_in = both(in_keep, swap(in_send, "hidden"), "hidden")
        d_down, d_up, d_cross, d_self = (d[0].astype(F32) for d in (d_down, d_up, d_cross, d_self))
        d_small = d_self[:, :, 1536:]
        columns = jnp.concatenate([d_small[i, :13, 16 * (i % 8) : 16 * (i % 8) + 16].T for i in range(BLOCKS)])
        d_unit = jnp.concatenate([d_small[i, 13, 64 * (i % 2) : 64 * (i % 2) + 64] for i in range(BLOCKS)])
        d_cross = d_cross.reshape(D, 2560)
        rest = tuple(
            lax.psum_scatter(d, BOTH, scatter_dimension=0, tiled=True)
            for d in (
                d_self[:, :, :1536].reshape(D, 1536), d_cross[:, 2048:], d_cross[:, :512], d_cross[:, 512:1536],
                d_cross[:, 1536:2048], d_up.transpose(0, 2, 1, 3).reshape(D, FF), d_down.reshape(FF, D), columns[:, 10:], columns[:, :10],
                d_unit,
            )
        )
    return (output, grad_hidden_in, grad_memory) + rest


def solution(mesh):
    rows = P(BOTH, None)
    part = P("batch", "seq", None)
    return jax.shard_map(
        functools.partial(per_device, mesh.devices.size),
        mesh=mesh,
        in_specs=(part, part, P("batch"), P("batch", None), part) + (rows,) * 9 + (P(BOTH),),
        out_specs=(part, part, part) + (rows,) * 9 + (P(BOTH),),
        check_vma=False,
    )
```

```python
import functools

import jax
import jax.numpy as jnp
from jax import lax
from jax.experimental import pallas as pl
from jax.experimental.pallas import tpu as pltpu
from jax.sharding import PartitionSpec as P

D = 512
FF = 2048
HEADS = 8
HEAD_DIM = 64
EPSILON = 1e-05
NEGATIVE = -1000000000.0
SCALE = HEAD_DIM ** (-0.5)
BLOCKS = 32
WIDE = 4096
BF = jnp.bfloat16
F32 = jnp.float32
BOTH = ("batch", "seq")

QKV, OUT, CQ, CKV, CO = (0, 1536), (1536, 2048), (2048, 2560), (2560, 3584), (3584, 4096)


def dot(a, b):
    return lax.dot_general(a, b, (((1,), (0,)), ((), ())), preferred_element_type=F32)


def dot_nt(a, b):
    return lax.dot_general(a, b, (((1,), (1,)), ((), ())), preferred_element_type=F32)


def dot_tn(a, b):
    return lax.dot_general(a, b, (((0,), (0,)), ((), ())), preferred_element_type=F32)


def norm(values):
    centred = values - jnp.mean(values, axis=-1, keepdims=True)
    rate = lax.rsqrt(jnp.mean(centred * centred, axis=-1, keepdims=True) + EPSILON)
    return centred * rate, rate


def norm_back(values, gain, grad):
    unit, rate = norm(values)
    scaled = grad * gain
    part = rate * (
        scaled
        - jnp.mean(scaled, axis=-1, keepdims=True)
        - unit * jnp.mean(scaled * unit, axis=-1, keepdims=True)
    )
    return part, row_sum(grad * unit), row_sum(grad)


def row_sum(values):
    return jnp.sum(values.astype(F32), axis=0, keepdims=True)


def lane_masks(dtype):
    lane = lax.broadcasted_iota(jnp.int32, (1, 128), 1)
    return [(lane // HEAD_DIM == j).astype(dtype) for j in range(2)]


def scores_t(keys, queries, visible):
    return jnp.where(visible, dot_nt(keys, queries) * SCALE, NEGATIVE)


def attend(q_ref, k_ref, v_ref, visible, mixed_ref, probs_ref):
    masks = lane_masks(BF)
    for pair in range(HEADS // 2):
        cols = slice(128 * pair, 128 * pair + 128)
        queries, keys, values = q_ref[:, cols], k_ref[:, cols], v_ref[:, cols]
        total = None
        for j in range(2):
            scores = scores_t(keys, queries * masks[j], visible)
            top = jnp.max(scores, axis=0, keepdims=True)
            exponent = jnp.exp(scores - top)
            row_total = jnp.sum(exponent, axis=0, keepdims=True)
            probs = (exponent * (1.0 / row_total)).astype(BF)
            probs_ref[2 * pair + j] = probs
            part = dot_tn(probs, values * masks[j])
            total = part if total is None else total + part
        mixed_ref[:, cols] = total.astype(BF)


def attend_back(q_ref, k_ref, v_ref, probs_ref, mixed_ref, grad_ref, dq_ref, dk_ref, dv_ref):
    masks = lane_masks(BF)
    product = grad_ref[...].astype(F32) * mixed_ref[...].astype(F32)
    high = product.astype(BF)
    low = (product - high.astype(F32)).astype(BF)
    head = lax.broadcasted_iota(jnp.int32, (HEADS, D), 0)
    picks = (lax.broadcasted_iota(jnp.int32, (HEADS, D), 1) // HEAD_DIM == head).astype(BF)
    inner = dot_nt(picks, high) + dot_nt(picks, low)
    for pair in range(HEADS // 2):
        cols = slice(128 * pair, 128 * pair + 128)
        queries, keys, values, grads = q_ref[:, cols], k_ref[:, cols], v_ref[:, cols], grad_ref[:, cols]
        dq = dk = dv = None
        for j in range(2):
            own_q, own_k, own_g = queries * masks[j], keys * masks[j], grads * masks[j]
            probs = probs_ref[2 * pair + j]
            grad_probs = dot_nt(values, own_g)
            part_v = dot(probs, own_g)
            low = (probs.astype(F32) * (grad_probs - inner[2 * pair + j : 2 * pair + j + 1, :])).astype(BF)
            part_k = dot(low, own_q)
            part_q = dot_tn(low, own_k)
            dq = part_q if dq is None else dq + part_q
            dk = part_k if dk is None else dk + part_k
            dv = part_v if dv is None else dv + part_v
        dq_ref[:, cols] = (dq * SCALE).astype(BF)
        dk_ref[:, cols] = (dk * SCALE).astype(BF)
        dv_ref[:, cols] = dv.astype(BF)


def place_blocks(order, base, pieces, put):
    for i, piece in enumerate(pieces):
        if piece is None:
            continue
        count = piece.shape[0]

        @pl.loop(0, count)
        def _(b, piece=piece, first=base + i * count):
            put(piece, b, order[first + b])


def rows16(index):
    return pl.ds(pl.multiple_of(index * 16, 16), 16)


def halves(ref, place, rows):
    own = pl.ds(pl.multiple_of(place * rows, rows), rows)
    other = pl.ds(pl.multiple_of((1 - place) * rows, rows), rows)
    return ref.at[own], ref.at[other]


def self_visible(length, rows):
    key = lax.broadcasted_iota(jnp.int32, (rows, rows), 0)
    query = lax.broadcasted_iota(jnp.int32, (rows, rows), 1)
    return (key <= query) & (key < length)


def cross_visible(mask):
    row = jnp.broadcast_to(mask[...].astype(F32), (8, mask.shape[1]))
    column = row.T[:, 0:1]
    return (column > 0) | (lax.broadcasted_iota(jnp.int32, column.shape, 0) == 0)


def pack_kernel(
    me, all_lengths, all_units, gains, biases, qkv, out, cq, ckv, co, up, down, hidden, memory, grads, masks,
    order, info, attention, w_up, w_down, sent, kept, mask, token, rows, gain_rows, bias_rows, lengths, units, sems,
):
    index = me[0]
    core = (index // 2) % 2
    place = index % 2
    far = 1 - place
    moves = [(gains, gain_rows), (biases, bias_rows), (masks.at[pl.ds(place, 1)], mask), (up, w_up), (down, w_down)]
    moves += [(all_lengths, lengths), (all_units, units)]
    first = 0
    for part in (hidden, memory, grads):
        last = first + part.shape[1]
        moves.append((part.at[far], sent.at[first:last]))
        moves.append((part.at[place], kept.at[first:last]))
        first = last
    first = 0
    for part in (qkv, out, cq, ckv, co):
        width = part.shape[1]
        moves.append((part, attention.at[0, :, first : first + width]))
        first += width
    moves = [pltpu.make_async_copy(a, b, sems.at[i]) for i, (a, b) in enumerate(moves)]
    for move in moves:
        move.start()
    info[0] = place
    for kind, both in enumerate(FLIPS):
        for k in range(16):
            plane = [sum(((k >> b) & 1) * flip for b, flip in enumerate(flips)) for flips in both]
            order[BLOCKS * kind + k] = index ^ jnp.where(core == 0, plane[0], plane[1])
            order[BLOCKS * kind + 16 + k] = index ^ jnp.where(core == 0, plane[1] | 2, plane[0] | 2)
    token[...] = jnp.zeros_like(token)
    rows[...] = jnp.zeros_like(rows)
    lane = lax.broadcasted_iota(jnp.int32, (16, 128), 1)
    spread = (lane % 16 == lax.broadcasted_iota(jnp.int32, (16, 128), 0)).astype(BF)
    unit_lane = lax.broadcasted_iota(jnp.int32, (64, 128), 1)
    unit_spread = (unit_lane % 64 == lax.broadcasted_iota(jnp.int32, (64, 128), 0)).astype(BF)
    for move in moves:
        move.wait()
    info[1] = lengths[place]
    rows[13:14, :] = dot(jnp.broadcast_to(units[...], (16, 64)), unit_spread)[0:1, :]
    rows[0:10, :] = dot_tn(bias_rows[...], spread)
    rows[10:13, :] = dot(gain_rows[...], spread)
    attention[0, :, WIDE : WIDE + 128] = rows[...].astype(BF)


def join_kernel(have, got, extra, joined):
    count = have.shape[0]
    joined[0:count] = have[...]
    joined[count:] = got[...]


def pass_kernel(value, out):
    out[...] = value[...]


def add_kernel(axis, *refs):
    *parts, send, keep = refs
    count = send.shape[0]
    first = 0
    for own, got in zip(parts[::2], parts[1::2]):
        last = first + own.shape[axis]
        place = (slice(None),) * axis + (slice(first, last),)
        send[place] = (own[count:].astype(F32) + got[count:].astype(F32)).astype(send.dtype)
        keep[place] = (own[:count].astype(F32) + got[:count].astype(F32)).astype(keep.dtype)
        first = last


def last_ffn_kernel(*refs):
    (*parts, d_up, d_down) = refs
    total = [own[0] + got[0].astype(F32) for own, got in zip(parts[::2], parts[1::2])]
    total = total[0] if len(total) == 1 else jnp.concatenate(total, axis=0)
    for group in range(4):
        d_up[:, 512 * group : 512 * group + 512] = total[group]
        d_down[16 * group : 16 * group + 16, :] = total[4 + group]


def last_attention_kernel(me, *refs):
    (*parts, d_cq, d_ckv, d_co, d_out, d_qkv, d_gains, d_biases, d_units) = refs
    total = [own[0] + got[0].astype(F32) for own, got in zip(parts[::2], parts[1::2])]
    total = total[0] if len(total) == 1 else jnp.concatenate(total, axis=1)
    d_cq[...] = total[:, 0:512]
    d_ckv[...] = total[:, 512:1536]
    d_co[...] = total[:, 1536:2048]
    d_out[...] = total[:, 2048:2560]
    d_qkv[...] = total[:, 2560:4096]
    small = total[:, 4096:4224]
    index = me[0]
    vectors = pltpu.roll(small, (128 - 16 * (index % 8)) % 128, 1)[:, 0:16]
    d_gains[...] = vectors[10:13, :]
    d_biases[...] = vectors.T[:, 0:10]
    d_units[...] = pltpu.roll(small, (128 - 64 * (index % 2)) % 128, 1)[13:14, 0:64]


def halves_kernel(info, kept, got, out):
    place = info[0]
    out[place] = kept[...]
    out[1 - place] = got[...].astype(out.dtype)


def self_forward_kernel(
    base, order, info, p0, p1, p2, p3, kept, new, weights, vecs, ffb, x0, normed1, q, k, v, mixed1, probs1, x1, normed2,
    small,
):
    place, length = info[0], info[1]

    def put(piece, b, index):
        weights[rows16(index), :] = piece[b, :, 0:2048]
        small[index] = piece[b, :, WIDE : WIDE + 128]

    place_blocks(order, base, (p0, p1, p2, p3), put)
    rows = x0.shape[0] // 2
    own, other = halves(x0, place, rows)
    own[...], other[...] = kept[0:rows], new[0:rows]
    hidden = x0[...].astype(F32)
    lane = lax.broadcasted_iota(jnp.int32, (16, 128), 1)
    for tile in range(D // 128):
        row = jnp.zeros((16, 128), F32)
        for i in range(8):
            row = jnp.where(lane // 16 == i, small[8 * tile + i].astype(F32), row)
        vecs[:, 128 * tile : 128 * tile + 128] = row
    ffb[...] = jnp.zeros_like(ffb)
    for tile in range(FF // 128):
        row = jnp.where(lane < 64, small[2 * tile].astype(F32), small[2 * tile + 1].astype(F32))
        ffb[tile // 4 : tile // 4 + 1, 128 * (tile % 4) : 128 * (tile % 4) + 128] = row[13:14, :]

    def bias(j):
        return vecs[j : j + 1, :]

    normed1[...] = (norm(hidden)[0] * bias(10) + bias(0)).astype(BF)
    q[...] = (dot(normed1[...], weights[:, 0:512]) + bias(1)).astype(BF)
    k[...] = dot(normed1[...], weights[:, 512:1024]).astype(BF)
    v[...] = (dot(normed1[...], weights[:, 1024:1536]) + bias(2)).astype(BF)
    attend(q, k, v, self_visible(length, 2 * rows), mixed1, probs1)
    after_self = hidden + (dot(mixed1[...], weights[:, 1536:2048]) + bias(3))
    x1[...] = after_self
    normed2[...] = (norm(after_self)[0] * bias(11) + bias(4)).astype(BF)


def cross_forward_kernel(
    base, order, info, p0, p1, p2, p3, kept, new, mask, vecs, x1, normed2,
    weights, mem, cq, ck, cv, mixed2, probs2, x2, normed3,
):
    place = info[0]

    def put(piece, b, index):
        weights[rows16(index), :] = piece[b, :, 2048:4096]

    place_blocks(order, base, (p0, p1, p2, p3), put)
    sources = mem.shape[0] // 2
    first = x1.shape[0] // 2
    own, other = halves(mem, place, sources)
    own[...], other[...] = kept[first : first + sources], new[first : first + sources]

    def bias(j):
        return vecs[j : j + 1, :]

    ck[...] = dot(mem[...], weights[:, 512:1024]).astype(BF)
    cv[...] = (dot(mem[...], weights[:, 1024:1536]) + bias(6)).astype(BF)
    cq[...] = (dot(normed2[...], weights[:, 0:512]) + bias(5)).astype(BF)
    attend(cq, ck, cv, cross_visible(mask), mixed2, probs2)
    after_cross = x1[...] + (dot(mixed2[...], weights[:, 1536:2048]) + bias(7))
    x2[...] = after_cross
    normed3[...] = (norm(after_cross)[0] * bias(12) + bias(8)).astype(BF)


def four_rows(index):
    return pl.ds(pl.multiple_of(index * 4, 4), 4)


def ffn_kernel(
    bases, order, info, u0, u1, u2, u3, w0, w1, w2, w3, x2, normed3, kept, new, vecs, ffb,
    out_keep, out_send, up, grad_hidden, grad_out, own_out, other_out,
    down, d_down, result,
):
    place = info[0]

    def put_up(piece, b, index):
        up[rows16(index), :] = piece[b]

    def put_down(piece, b, index):
        down[four_rows(index)] = piece[b]

    place_blocks(order, bases[0], (u0, u1, u2, u3), put_up)
    place_blocks(order, bases[1], (w0, w1, w2, w3), put_down)
    rows = out_keep.shape[0]
    first = kept.shape[0] - rows
    own, other = halves(grad_out, place, rows)
    own[...], other[...] = kept[first:], new[first:]
    grads = grad_out[...]
    normed = normed3[...]
    total = None
    c0 = (2.0 / jnp.pi) ** 0.5
    for group in range(FF // 512):
        w_down = down[32 * group : 32 * group + 32].reshape(512, D)
        hidden = dot(normed, up[:, 512 * group : 512 * group + 512]) + ffb[group : group + 1, :]
        square = hidden * hidden
        tanh = jnp.tanh(c0 * (hidden + 0.044715 * (square * hidden)))
        half = 0.5 * (1.0 + tanh)
        active = (hidden * half).astype(BF)
        slope = half + hidden * (0.5 * c0) * (1.0 - tanh * tanh) * (1.0 + (3 * 0.044715) * square)
        part = dot(active, w_down)
        total = part if total is None else total + part
        grad_hidden[:, 512 * group : 512 * group + 512] = (slope * dot_nt(grads, w_down)).astype(BF)
        d_down[32 * group : 32 * group + 32] = dot_tn(active, grads).astype(BF).reshape(32, 16, D)
    take_blocks(order, bases[2], (own_out, other_out), lambda index: d_down[four_rows(index)])
    result[...] = (x2[...] + (total + vecs[9:10, :])).astype(BF)
    own, other = halves(result, place, rows)
    out_keep[...], out_send[...] = own[...], other[...]


def ffn_back_kernel(
    base, order, info, up, grad_hidden, grad_out, x2, normed3, vecs, grad_x2, small, ffg, own_out, other_out, d_up
):
    normed_t = normed3[...].T
    grad_normed = None
    ffg[...] = jnp.zeros_like(ffg)
    for group in range(FF // 512):
        grad = grad_hidden[:, 512 * group : 512 * group + 512]
        d_up[group] = dot(normed_t, grad).astype(BF)
        ffg[group : group + 1, :] = row_sum(grad)
        part = dot_nt(grad, up[:, 512 * group : 512 * group + 512])
        grad_normed = part if grad_normed is None else grad_normed + part
    take_blocks(order, base, (own_out, other_out), lambda index: d_up[:, rows16(index), :])
    part, d_gain, d_shift = norm_back(x2[...], vecs[12:13, :], grad_normed)
    grads = grad_out[...]
    grad_x2[...] = grads.astype(F32) + part
    small[...] = jnp.zeros_like(small)
    small[12:13, :] = d_gain
    small[8:9, :] = d_shift
    small[9:10, :] = row_sum(grads)


def cross_back_kernel(
    base, order, info, weights, weights1, x1, normed2, mem, cq, ck, cv, mixed1, mixed2, probs2, grad_x2, vecs, small_in,
    grad_x1, grad_mixed1, mem_keep, mem_send, small, own_out, other_out,
    d_weights, grad_mixed, dq, dk, dv, grad_mem,
):
    place = info[0]
    small[...] = small_in[...]
    grad_y = grad_x2[...].astype(BF)
    d_weights[:, 1536:2048] = dot_tn(mixed2[...], grad_y).astype(BF)
    small[7:8, :] = row_sum(grad_y)
    grad_mixed[...] = dot_nt(grad_y, weights[:, 1536:2048]).astype(BF)
    attend_back(cq, ck, cv, probs2, mixed2, grad_mixed, dq, dk, dv)
    memory_t = mem[...].T
    d_weights[:, 512:1024] = dot(memory_t, dk[...]).astype(BF)
    d_weights[:, 1024:1536] = dot(memory_t, dv[...]).astype(BF)
    d_weights[:, 0:512] = dot_tn(normed2[...], dq[...]).astype(BF)
    small[6:7, :] = row_sum(dv[...])
    small[5:6, :] = row_sum(dq[...])
    grad_mem[...] = dot_nt(dk[...], weights[:, 512:1024]) + dot_nt(dv[...], weights[:, 1024:1536])
    own, other = halves(grad_mem, place, mem_keep.shape[0])
    mem_keep[...] = own[...]
    mem_send[...] = other[...].astype(BF)
    part, d_gain, d_shift = norm_back(x1[...], vecs[11:12, :], dot_nt(dq[...], weights[:, 0:512]))
    small[11:12, :] = d_gain
    small[4:5, :] = d_shift
    total = grad_x2[...] + part
    grad_x1[...] = total
    grad_y = total.astype(BF)
    d_weights[:, 2048:2560] = dot_tn(mixed1[...], grad_y).astype(BF)
    small[3:4, :] = row_sum(grad_y)
    grad_mixed1[...] = dot_nt(grad_y, weights1[:, 1536:2048]).astype(BF)
    take_blocks(order, base, (own_out, other_out), lambda index: d_weights[rows16(index), :])


def self_back_kernel(
    base, order, info, weights, x0, normed1, q, k, v, mixed1, probs1, grad_x1, grad_mixed, vecs, small_in, ffg,
    in_keep, in_send, own_out, other_out,
    d_weights, d_small, small, dq, dk, dv, grad_in,
):
    place = info[0]
    small[...] = small_in[...]
    rows = q.shape[0]
    attend_back(q, k, v, probs1, mixed1, grad_mixed, dq, dk, dv)
    normed_t = normed1[...].T
    for i, part in enumerate((dq, dk, dv)):
        d_weights[:, 512 * i : 512 * i + 512] = dot(normed_t, part[...]).astype(BF)
    small[1:2, :] = row_sum(dq[...])
    small[2:3, :] = row_sum(dv[...])
    grad_normed = (
        dot_nt(dq[...], weights[:, 0:512])
        + dot_nt(dk[...], weights[:, 512:1024])
        + dot_nt(dv[...], weights[:, 1024:1536])
    )
    part, d_gain, d_shift = norm_back(x0[...].astype(F32), vecs[10:11, :], grad_normed)
    small[10:11, :] = d_gain
    small[0:1, :] = d_shift
    for index in range(BLOCKS):
        tile = 128 * (index // 8)
        d_small[index] = small[:, tile : tile + 128].astype(BF)
        group, tile = index // 8, 128 * ((index // 2) % 4)
        d_small[index, 13:14, :] = ffg[group : group + 1, tile : tile + 128].astype(BF)
    first = base
    for out in (own_out, other_out):
        if out is None:
            continue

        @pl.loop(0, out.shape[0])
        def _(b, out=out, first=first):
            index = order[first + b]
            out[b, :, 0:1536] = d_weights[rows16(index), :]
            out[b, :, 1536:1664] = d_small[index]

        first += out.shape[0]
    grad_in[...] = grad_x1[...] + part
    own, other = halves(grad_in, place, rows // 2)
    in_keep[...] = own[...]
    in_send[...] = other[...].astype(BF)


def take_blocks(order, base, outs, take):
    first = base
    for out in outs:
        if out is None:
            continue

        @pl.loop(0, out.shape[0])
        def _(b, out=out, first=first):
            out[b] = take(order[first + b])

        first += out.shape[0]


VMEM = pl.BlockSpec(memory_space=pltpu.VMEM)
SMEM = pl.BlockSpec(memory_space=pltpu.SMEM)
HBM = pl.BlockSpec(memory_space=pltpu.HBM)


def shape(dims, dtype):
    return jax.ShapeDtypeStruct(dims, dtype)


EVENT = 1_000_000_000


class Line:
    def __init__(self):
        self.token = None

    def call(self, kernel, name, inputs, outs, scratch=(), scalars=0, flops=1):
        given = [i for i in inputs if i is not None]
        made = [o for o in outs if o is not None]
        tokens = [self.token] if self.token is not None else []

        def body(*refs):
            refs = list(refs)
            taken = [None if i is None else refs.pop(0) for i in inputs]
            for _ in tokens:
                refs.pop(0)
            given_out = [None if o is None else refs.pop(0) for o in outs]
            out_token = refs.pop(0)
            out_token[...] = jnp.zeros_like(out_token)
            kernel(*taken, *given_out, *refs)

        moved = sum(a.size * a.dtype.itemsize for a in given)
        *results, self.token = pl.pallas_call(
            body,
            name=name,
            out_shape=[shape(*o) for o in made] + [shape((8, 128), F32)],
            in_specs=[SMEM] * scalars + [VMEM] * (len(given) - scalars + len(tokens)),
            out_specs=[VMEM] * (len(made) + 1),
            scratch_shapes=list(scratch),
            compiler_params=pltpu.CompilerParams(vmem_limit_bytes=32 * 1024 * 1024),
            cost_estimate=pl.CostEstimate(flops=flops, bytes_accessed=1, transcendentals=0),
        )(*given, *tokens)
        results = iter(results)
        return [None if o is None else next(results) for o in outs]


def flat_index(z, y, c, x):
    return ((z * 2 + y) * 2 + c) * 2 + x


def pairs_of(move):
    pairs = []
    for z in range(4):
        for y in range(2):
            for c in range(2):
                for x in range(2):
                    pairs.append((flat_index(z, y, c, x), flat_index(*move(z, y, c, x))))
    return pairs


CORE = pairs_of(lambda z, y, c, x: (z, y, 1 - c, x))
SIDE = pairs_of(lambda z, y, c, x: (z, y, c, 1 - x))
HOP_Z1 = pairs_of(lambda z, y, c, x: (z ^ 1 if c == 0 else z ^ 2, y, c, x))
HOP_Z2 = pairs_of(lambda z, y, c, x: (z ^ 2 if c == 0 else z ^ 1, y, c, x))
HOP_P1 = pairs_of(lambda z, y, c, x: (z, y, c, 1 - x) if c == 0 else (z, 1 - y, c, x))
HOP_P2 = pairs_of(lambda z, y, c, x: (z, y, c, 1 - x) if c == 1 else (z, 1 - y, c, x))
HOPS = (
    (HOP_Z1, HOP_Z2, HOP_P1, HOP_P2),
    (HOP_P1, HOP_P2, HOP_Z1, HOP_Z2),
    (HOP_P1, HOP_Z1, HOP_Z2, HOP_P2),
)
FLIPS = (
    ((8, 16, 1, 4), (16, 8, 4, 1)),
    ((1, 4, 8, 16), (4, 1, 16, 8)),
    ((1, 8, 16, 4), (4, 16, 8, 1)),
)
GATHER_KIND = dict(a=0, u=0, w=1)
GATHER = (
    ("a", 12), ("w", 12), ("u", 12), ("a", 12), ("w", 12), ("u", 12), ("a", 12), ("w", 12), ("u", 12),
)
SCATTER_KIND = dict(d=2, u=2, f=2, c=0, s=0, a=0)
SCATTER = (
    ("d", 0), ("u", 0), ("X", 0), ("Y", 0), ("d", 12), ("u", 0), ("c", 3),
    ("s", 0), ("d", 0.3), ("o", 4), ("s", 0.6), ("c", 0), ("u", 0), ("s", 0.3),
    ("d", 1.5), ("c", 0), ("u", 0), ("s", 1.5), ("c", 0), ("m", 0), ("udf", 0),
    ("f", 0.6), ("h", 0), ("csa", 0), ("a", 0),
)


def permute(value, pairs):
    return lax.ppermute(value, BOTH, pairs)


class Gather:
    def __init__(self, line, name, own):
        self.line, self.name, self.have, self.hop = line, name, own, 0
        self.hops = HOPS[GATHER_KIND[name]]

    def start(self):
        with jax.named_scope(f"gather_{self.name}_hop{self.hop}"):
            self.coming = permute(self.have, self.hops[self.hop])
        self.hop += 1
        if self.hop == 4:
            with jax.named_scope(f"gather_{self.name}_core0"):
                self.core = permute(self.have, CORE)

    def step(self, extra, cost):
        dims = self.have.shape
        (self.have,) = self.line.call(
            join_kernel, f"join_{self.name}{self.hop}", [self.have, self.coming, extra],
            [((2 * dims[0],) + dims[1:], BF)], flops=cost,
        )
        self.start()

    def finish(self, tied=False):
        if tied:
            (self.coming,) = self.line.call(
                pass_kernel, f"pass_{self.name}", [self.coming], [(self.coming.shape, BF)], flops=12 * EVENT
            )
        with jax.named_scope(f"gather_{self.name}_core1"):
            return [self.have, self.coming, self.core, permute(self.coming, CORE)]


class Scatter:
    def __init__(self, line, name, hop, parts):
        self.line, self.name, self.hop, self.parts = line, name, hop, parts
        self.hops, self.axis = HOPS[SCATTER_KIND[name]], (1 if name in "duf" else 2)

    @classmethod
    def begin(cls, line, name, own, other):
        with jax.named_scope(f"scatter_{name}_core"):
            return cls(line, name, 4, [(own, permute(other, CORE))])

    def step(self, cost):
        self.hop -= 1
        dims = list(self.parts[0][0].shape)
        dims[0], dims[self.axis] = 1 << self.hop, sum(own.shape[self.axis] for own, _ in self.parts)
        send, own = self.line.call(
            functools.partial(add_kernel, self.axis), f"add_{self.name}{self.hop}", [v for p in self.parts for v in p],
            [(tuple(dims), BF), (tuple(dims), BF if self.hop else F32)], flops=cost,
        )
        with jax.named_scope(f"scatter_{self.name}_hop{self.hop}"):
            self.parts = [(own, permute(send, self.hops[self.hop]))]


def small_rows(biases, gains, ffn_bias):
    count = biases.shape[0]
    columns = jnp.concatenate([biases, gains], axis=2).transpose(0, 2, 1)
    rows = jnp.tile(columns, (1, 1, 8))
    units = jnp.tile(ffn_bias.reshape(count, 1, 64), (1, 1, 2))
    return jnp.concatenate([rows, units, jnp.zeros((count, 2, 128), BF)], axis=1)


def pack_attention(qkv, out, cq, ckv, co, small):
    return jnp.concatenate([qkv, out, cq, ckv, co, small], axis=2)


def packed(hidden_in, memory, lengths, source_mask, grad_out, params, me):
    (w_qkv, w_out, w_cq, w_ckv, w_co, w_up, w_down, gains, biases, ffn_bias) = params
    rows = 2 * hidden_in.shape[1] + memory.shape[1]
    return pl.pallas_call(
        pack_kernel,
        name="pack",
        out_shape=[
            shape((len(FLIPS) * BLOCKS,), jnp.int32), shape((2,), jnp.int32), shape((1, 16, WIDE + 128), BF),
            shape((16, FF), BF), shape((64, D), BF), shape((rows, D), BF), shape((rows, D), BF),
            shape((1, source_mask.shape[1]), jnp.int32), shape((8, 128), F32),
        ],
        in_specs=[SMEM] + [HBM] * 15,
        out_specs=[SMEM, SMEM] + [VMEM] * 7,
        scratch_shapes=[
            pltpu.VMEM((16, 128), F32), pltpu.VMEM((3, 16), BF), pltpu.VMEM((16, 10), BF),
            pltpu.SMEM(lengths.shape, jnp.int32), pltpu.VMEM((1, 64), BF), pltpu.SemaphoreType.DMA((18,)),
        ],
        compiler_params=pltpu.CompilerParams(vmem_limit_bytes=16 * 1024 * 1024),
    )(
        me,
        *(
            pltpu.with_memory_space_constraint(v, pltpu.HBM)
            for v in (
                lengths, ffn_bias.reshape(1, 64), gains.T, biases, w_qkv, w_out, w_cq, w_ckv, w_co, w_up, w_down, hidden_in, memory, grad_out, source_mask,
            )
        ),
    )


def per_device(n_devices, hidden_in, memory, lengths, source_mask, grad_out, *params):
    permuted = n_devices == BLOCKS
    rows, sources = hidden_in.shape[1], memory.shape[1]
    tgt, src = 2 * rows, 2 * sources
    line = Line()

    def swap(value, name):
        with jax.named_scope(f"swap_{name}"):
            return lax.ppermute(value, "seq", [(0, 1), (1, 0)])

    place = lax.axis_index("seq")
    if permuted:
        me = lax.axis_index(BOTH).astype(jnp.int32).reshape(1)
        order, info, attention, w_up, w_down, sent, kept, mask, line.token = packed(
            hidden_in, memory, lengths, source_mask, grad_out, params, me
        )
        chunks = dict(
            a=Gather(line, "a", attention), w=Gather(line, "w", w_down.reshape(1, 4, 16, D)),
            u=Gather(line, "u", w_up[None]),
        )
        chunks["a"].start()
        chunks["w"].start()
        new = swap(sent, "in")
        chunks["u"].start()
        for name, cost in GATHER:
            chunks[name].step(new if name == "a" and chunks[name].hop == 2 else None, int(cost * EVENT))
        a_pieces = chunks["a"].finish()
        halves_of = (16, 16)
        base = lambda kind: BLOCKS * kind
    else:
        params = [lax.all_gather(p, BOTH, axis=0, tiled=True) for p in params]
        (w_qkv, w_out, w_cq, w_ckv, w_co, w_up, w_down, gains, biases, ffn_bias) = params
        cut = lambda w: w.reshape(BLOCKS, -1, w.shape[1])
        attention = pack_attention(
            *(cut(w) for w in (w_qkv, w_out, w_cq, w_ckv, w_co)), small_rows(cut(biases), cut(gains), ffn_bias)
        )
        pick = lambda v, i: lax.dynamic_index_in_dim(v, i, 0, keepdims=False)
        both_of = lambda i: jnp.concatenate([pick(v, i) for v in (hidden_in, memory, grad_out)], axis=0)
        kept, new = both_of(place), swap(both_of(1 - place), "in")
        mask = pick(source_mask, place)[None]
        info = jnp.stack([place, pick(lengths, place)]).astype(jnp.int32)
        order = jnp.arange(BLOCKS, dtype=jnp.int32)
        a_pieces = [attention, None, None, None]
        halves_of = (BLOCKS, None)
        base = lambda kind: 0

    wide = (tgt, D)
    vec = ((16, D), F32)
    units = ((8, 512), F32)
    blocks = lambda *dims: [None if n is None else ((n,) + dims, BF) for n in halves_of]
    weights1, vecs, ffb, x0, normed1, q, k, v, mixed1, probs1, x1, normed2 = line.call(
        functools.partial(self_forward_kernel, base(GATHER_KIND["a"])), "self_forward", [order, info, *a_pieces, kept, new],
        [
            ((D, 2048), BF), vec, units, (wide, BF), (wide, BF), (wide, BF), (wide, BF), (wide, BF), (wide, BF),
            ((HEADS, tgt, tgt), BF), (wide, F32), (wide, BF),
        ],
        [pltpu.VMEM((BLOCKS, 16, 128), BF)], 2,
    )
    if permuted:
        w_pieces = chunks["w"].finish()
    weights2, mem, cq, ck, cv, mixed2, probs2, x2, normed3 = line.call(
        functools.partial(cross_forward_kernel, base(GATHER_KIND["a"])), "cross_forward",
        [order, info, *a_pieces, kept, new, mask, vecs, x1, normed2],
        [
            ((D, 2048), BF), ((src, D), BF), (wide, BF), ((src, D), BF), ((src, D), BF), (wide, BF),
            ((HEADS, src, tgt), BF), (wide, F32), (wide, BF),
        ],
        [], 2,
    )
    if permuted:
        u_pieces = chunks["u"].finish(True)
    else:
        u_pieces, w_pieces = [cut(w_up), None, None, None], [w_down.reshape(BLOCKS, 4, 16, D), None, None, None]
    bases = (base(GATHER_KIND["u"]), base(GATHER_KIND["w"]), base(SCATTER_KIND["d"]))
    out_keep, out_send, up, grad_hidden, g_full, *d_down = line.call(
        functools.partial(ffn_kernel, bases), "ffn",
        [order, info, *u_pieces, *w_pieces, x2, normed3, kept, new, vecs, ffb],
        [((rows, D), BF), ((rows, D), BF), ((D, FF), BF), ((tgt, FF), BF), (wide, BF), *blocks(4, 16, D)],
        [pltpu.VMEM((128, 16, D), BF), pltpu.VMEM((128, 16, D), BF), pltpu.VMEM(wide, BF)], 2,
    )
    if permuted:
        chunks = dict(d=Scatter.begin(line, "d", *d_down))
        out_got = swap(out_send, "out")
    grad_x2, small, ffg, *d_up = line.call(
        functools.partial(ffn_back_kernel, base(SCATTER_KIND["u"])), "ffn_back",
        [order, info, up, grad_hidden, g_full, x2, normed3, vecs],
        [(wide, F32), vec, units, *blocks(4, 16, 512)],
        [pltpu.VMEM((4, D, 512), BF)], 2,
    )

    def cross_back():
        return line.call(
            functools.partial(cross_back_kernel, base(SCATTER_KIND["c"])), "cross_back",
            [
                order, info, weights2, weights1, x1, normed2, mem, cq, ck, cv, mixed1, mixed2, probs2, grad_x2, vecs,
                small,
            ],
            [(wide, F32), (wide, BF), ((sources, D), F32), ((sources, D), BF), vec, *blocks(16, 2560)],
            [
                pltpu.VMEM((D, 2560), BF), pltpu.VMEM(wide, BF), pltpu.VMEM(wide, BF),
                pltpu.VMEM((src, D), BF), pltpu.VMEM((src, D), BF), pltpu.VMEM((src, D), F32),
            ],
            2,
        )

    def self_back(grad_x1, grad_mixed1, small):
        return line.call(
            functools.partial(self_back_kernel, base(SCATTER_KIND["s"])), "self_back",
            [order, info, weights1, x0, normed1, q, k, v, mixed1, probs1, grad_x1, grad_mixed1, vecs, small, ffg],
            [((rows, D), F32), ((rows, D), BF), *blocks(16, 1664)],
            [
                pltpu.VMEM((D, 1536), BF), pltpu.VMEM((BLOCKS, 16, 128), BF), pltpu.VMEM((16, D), F32),
                pltpu.VMEM(wide, BF), pltpu.VMEM(wide, BF), pltpu.VMEM(wide, BF), pltpu.VMEM(wide, F32),
            ],
            2,
        )

    def both(kept, got, name):
        return line.call(halves_kernel, f"halves_{name}", [info, kept, got], [((2,) + kept.shape, kept.dtype)], (), 1)[0]

    if permuted:
        chunks["u"] = Scatter.begin(line, "u", *d_up)
        lasts = dict(
            f=(last_ffn_kernel, [((16, FF), F32), ((64, D), F32)]),
            a=(
                last_attention_kernel,
                [((16, n), F32) for n in (512, 1024, 512, 512, 1536)]
                + [((3, 16), F32), ((16, 10), F32), ((1, 64), F32)],
            ),
        )
        done = {}
        for name, cost in SCATTER:
            if name == "X":
                grad_x1, grad_mixed1, mem_keep, mem_send, small, *d_cross = cross_back()
                chunks["c"] = Scatter.begin(line, "c", *d_cross)
                mem_got = swap(mem_send, "memory")
            elif name == "Y":
                in_keep, in_send, *d_self = self_back(grad_x1, grad_mixed1, small)
                chunks["s"] = Scatter.begin(line, "s", *d_self)
                in_got = swap(in_send, "hidden")
            elif name == "o":
                output = both(out_keep, out_got, "out")
            elif name == "m":
                grad_memory = both(mem_keep, mem_got, "memory")
            elif name == "h":
                grad_hidden_in = both(in_keep, in_got, "hidden")
            elif len(name) > 1:
                first, second, joined = name
                hop = chunks[first].hop
                chunks[joined] = Scatter(line, joined, hop, chunks[first].parts + chunks[second].parts)
            elif chunks[name].hop:
                chunks[name].step(int(cost * EVENT))
            else:
                kernel, shapes = lasts[name]
                mine = [me] if name == "a" else []
                done[name] = line.call(
                    kernel, f"last_{name}", mine + [v for p in chunks[name].parts for v in p], shapes,
                    scalars=len(mine), flops=int(cost * EVENT),
                )
        g_up, g_down = done["f"]
        g_cq, g_ckv, g_co, g_out, g_qkv, g_gains, g_biases, g_units = done["a"]
        rest = (g_qkv, g_out, g_cq, g_ckv, g_co, g_up, g_down, g_gains.T, g_biases, g_units.reshape(64))
    else:
        grad_x1, grad_mixed1, mem_keep, mem_send, small, *d_cross = cross_back()
        in_keep, in_send, *d_self = self_back(grad_x1, grad_mixed1, small)
        output = both(out_keep, swap(out_send, "out"), "out")
        grad_memory = both(mem_keep, swap(mem_send, "memory"), "memory")
        grad_hidden_in = both(in_keep, swap(in_send, "hidden"), "hidden")
        d_down, d_up, d_cross, d_self = (d[0].astype(F32) for d in (d_down, d_up, d_cross, d_self))
        d_small = d_self[:, :, 1536:]
        columns = jnp.concatenate([d_small[i, :13, 16 * (i % 8) : 16 * (i % 8) + 16].T for i in range(BLOCKS)])
        d_unit = jnp.concatenate([d_small[i, 13, 64 * (i % 2) : 64 * (i % 2) + 64] for i in range(BLOCKS)])
        d_cross = d_cross.reshape(D, 2560)
        rest = tuple(
            lax.psum_scatter(d, BOTH, scatter_dimension=0, tiled=True)
            for d in (
                d_self[:, :, :1536].reshape(D, 1536), d_cross[:, 2048:], d_cross[:, :512], d_cross[:, 512:1536],
                d_cross[:, 1536:2048], d_up.transpose(0, 2, 1, 3).reshape(D, FF), d_down.reshape(FF, D), columns[:, 10:], columns[:, :10],
                d_unit,
            )
        )
    return (output, grad_hidden_in, grad_memory) + rest


def solution(mesh):
    rows = P(BOTH, None)
    part = P("batch", "seq", None)
    return jax.shard_map(
        functools.partial(per_device, mesh.devices.size),
        mesh=mesh,
        in_specs=(part, part, P("batch"), P("batch", None), part) + (rows,) * 9 + (P(BOTH),),
        out_specs=(part, part, part) + (rows,) * 9 + (P(BOTH),),
        check_vma=False,
    )
```
